256 devices in a mesh: dp: 128 (over z, x, y_hi, core), mp: 2 (over y_lo).
Axes of the slice: x: 4, y: 4 (y_hi: 2, y_lo: 2; y = y_hi * 2 + y_lo), z: 8, core: 2. Of those that a mesh axis runs over, the one named last changes fastest.
Arguments:
- features: bfloat16 [256, 512, 768], P('dp'), may hold values from -24 to 24
- patch_counts: int32 [256], P('dp'), may hold values from 216 to 512, as said below
- ln1_gain: float32 [768], replicated, may hold values from 0.25 to 1.75
- ln1_bias: float32 [768], replicated, may hold values from -1.5 to 1.5
- query_key_value_weight: bfloat16 [768, 3, 768], P('dp', None, 'mp'), may hold values from -0.21875 to 0.21875
- qv_bias: float32 [2, 768], P(None, 'mp'), may hold values from -1.5 to 1.5
- out_weight: bfloat16 [768, 768], P('mp', 'dp'), may hold values from -3 to 3
- out_bias: float32 [768], replicated, may hold values from -1.5 to 1.5
- ln2_gain: float32 [768], replicated, may hold values from 0.25 to 1.75
- ln2_bias: float32 [768], replicated, may hold values from -1.5 to 1.5
- fc1_weight: bfloat16 [768, 3072], P('dp', 'mp'), may hold values from -0.21875 to 0.21875
- fc1_bias: float32 [3072], P('mp'), may hold values from -1.5 to 1.5
- fc2_weight: bfloat16 [3072, 768], P('mp', 'dp'), may hold values from -0.109375 to 0.109375
- fc2_bias: float32 [768], replicated, may hold values from -1.5 to 1.5
- cotangent: bfloat16 [256, 512, 768], P('dp'), may hold values from -24 to 24
Outputs:
- layer_out: bfloat16 [256, 512, 768], P('dp')
- features_grad: float32 [256, 512, 768], P('dp')
- ln1_gain_grad: float32 [768], replicated
- ln1_bias_grad: float32 [768], replicated
- qkv_weight_grad: float32 [768, 3, 768], P('dp', None, 'mp')
- qv_bias_grad: float32 [2, 768], P(None, 'mp')
- out_weight_grad: float32 [768, 768], P('mp', 'dp')
- out_bias_grad: float32 [768], replicated
- ln2_gain_grad: float32 [768], replicated
- ln2_bias_grad: float32 [768], replicated
- fc1_weight_grad: float32 [768, 3072], P('dp', 'mp')
- fc1_bias_grad: float32 [3072], P('mp')
- fc2_weight_grad: float32 [3072, 768], P('mp', 'dp')
- fc2_bias_grad: float32 [768], replicated
The draws below stay inside these ranges and needn't reach their ends.
Inputs may be any that keep to these rules, and one draw needn't show every extreme that they name: `patch_counts`: each item has 216, 256 or 512 valid patches, the first ones of its slots; both the smallest and the largest occur in every draw.
All inputs are finite; a program needn't handle non-finite values.
Results may differ from the reference program's by a relative error of at most 0.012.
Values may be sent and summed in bfloat16 or wider, within the bound.
No kernel may reach another device: no remote copies, remote signals or barrier semaphores. Data moves between devices by JAX's collectives and lax.ppermute only.
A program may use at most 128 MiB of HBM per device.

```python
import math
import jax
import jax.numpy as jnp
from jax import lax

D = 768
H = 12
DH = 64
FF = 3072
L = 512
ITEMS = 256


def draw_patch_counts(key, part):
    crop_kinds = jax.random.randint(jax.random.fold_in(key, 11), (ITEMS,), 0, 3)
    first_spot = jax.random.randint(jax.random.fold_in(key, 12), (), 0, ITEMS)
    step_spot = jax.random.randint(jax.random.fold_in(key, 13), (), 1, ITEMS)
    other_spot = (first_spot + step_spot) % ITEMS
    positions = jnp.arange(ITEMS)
    crop_kinds = jnp.where(positions == first_spot, 2, crop_kinds)
    crop_kinds = jnp.where(positions == other_spot, 0, crop_kinds)
    size_table = jnp.array([L * 27 // 64, L // 2, L], jnp.int32)
    return size_table[crop_kinds]


def spiked(values, stream_key, source, target, parts, factor):
    def block_of(dim):
        return (jnp.arange(values.shape[dim]) // (values.shape[dim] // parts)).reshape((-1,) + (1,) * (values.ndim - 1 - dim))

    near = jax.random.permutation(stream_key, parts)[block_of(target)]
    far = (block_of(target) + parts // 2) % parts
    return jnp.where((block_of(source) == near) | (block_of(source) == far), factor * values, values)


def levels(key, extent, split, smallest, top_value):
    level, own = 1.0, jax.random.fold_in(key, 6)
    for axis_at, parts in split:
        steps = jnp.exp(jax.random.uniform(jax.random.fold_in(own, axis_at), (parts,), jnp.float32, smallest / len(split), top_value / len(split)))
        level = level * jnp.repeat(steps, extent[axis_at] // parts).reshape([-1 if axis == axis_at else 1 for axis in range(len(extent))])
    return level


def bell_draw(rng, extent, deviation, bound, cuts=(), held_as=jnp.bfloat16):
    values = jax.random.normal(rng, extent, jnp.float32) * deviation
    if len(cuts) > 0:
        values = levels(rng, extent, cuts, -0.22, 0.18) * values
    return jnp.clip(values, min=-bound, max=bound).astype(held_as)


def bell_draw_with(key, shape, spread, most, split, heavy, held_as=jnp.bfloat16):
    drawn = spread * jax.random.normal(key, shape, jnp.float32)
    if split:
        drawn = drawn * levels(key, shape, split, -0.22, 0.18)
    return jnp.clip(spiked(drawn, jax.random.fold_in(key, 3), *heavy), -most, most).astype(held_as)


def setup_inputs(seed: int = 0) -> dict:
    key_list = jax.random.split(jax.random.key(seed), 16)
    return {
        "features": bell_draw_with(key_list[0], (ITEMS, L, D), 1.0, 24.0, ((0, 128),), (0, 2, 128, 5.5)),
        "patch_counts": draw_patch_counts(jax.random.fold_in(key_list[15], 71), 0),
        "ln1_gain": jnp.clip(1.0 + 0.15 * jax.random.normal(key_list[2], (D,), jnp.float32), 0.25, 1.75),
        "ln1_bias": bell_draw(key_list[3], (D,), 0.3, 1.5, (), jnp.float32),
        "query_key_value_weight": bell_draw(key_list[4], (D, 3, H * DH), D ** -0.5, 0.21875, ((0, 128), (2, 2))),
        "qv_bias": bell_draw(key_list[5], (2, H * DH), 0.3, 1.5, ((1, 2),), jnp.float32),
        "out_weight": bell_draw(key_list[6], (H * DH, D), 4 ** -0.5, 3.0, ((0, 2), (1, 128))),
        "out_bias": bell_draw(key_list[7], (D,), 0.3, 1.5, (), jnp.float32),
        "ln2_gain": jnp.clip(1.0 + 0.15 * jax.random.normal(key_list[8], (D,), jnp.float32), 0.25, 1.75),
        "ln2_bias": bell_draw(key_list[9], (D,), 0.3, 1.5, (), jnp.float32),
        "fc1_weight": bell_draw(key_list[10], (D, FF), D ** -0.5, 0.21875, ((0, 128), (1, 2))),
        "fc1_bias": bell_draw(key_list[11], (FF,), 0.3, 1.5, ((0, 2),), jnp.float32),
        "fc2_weight": bell_draw(key_list[12], (FF, D), FF ** -0.5, 0.109375, ((0, 2), (1, 128))),
        "fc2_bias": bell_draw(key_list[13], (D,), 0.3, 1.5, (), jnp.float32),
        "cotangent": bell_draw_with(key_list[14], (ITEMS, L, D), 1.0, 24.0, ((0, 128),), (0, 2, 128, 5.5)),
    }


@jax.custom_vjp
def low(v):
    return lax.optimization_barrier(v.astype(jnp.bfloat16)).astype(jnp.float32)

@jax.custom_vjp
def low_back(v):
    return v

def low_keep(v):
    return (low(v), None)

def low_pass(kept, grad):
    return (grad,)

def back_keep(v):
    return (v, None)

def back_low(kept, grad):
    return (low(grad),)
low.defvjp(low_keep, low_pass)
low_back.defvjp(back_keep, back_low)
top_precision = lax.Precision.HIGHEST
masked_score = -1e+30

def layer_norm(values, gain_row, shift_row):
    row_mean = lax.optimization_barrier(jnp.mean(values, axis=-1, keepdims=True))
    centred = values - row_mean
    variance = lax.optimization_barrier(jnp.mean(centred * centred, axis=-1, keepdims=True))
    return centred * lax.rsqrt(variance + 1e-06) * gain_row + shift_row

def block(feature_rows, count_rows, params):
    ln1_gain, ln1_bias, query_key_value_weight, qv_bias, out_weight, out_bias, ln2_gain, ln2_bias, fc1_weight, fc1_bias, fc2_weight, fc2_bias = params
    group_size, token_len, model_width = feature_rows.shape
    first_normalized = low(layer_norm(feature_rows, ln1_gain, ln1_bias))
    bias_row_block = jnp.stack([qv_bias[0], jnp.zeros_like(qv_bias[0]), qv_bias[1]])
    projected_rows = jnp.einsum('knx,xhp->knhp', first_normalized, query_key_value_weight, precision=top_precision) + bias_row_block
    qkv_low = low(low_back(projected_rows)).reshape(group_size, token_len, 3, H, DH)
    scores = jnp.einsum('gqhe,gkhe->ghqk', qkv_low[:, :, 0], qkv_low[:, :, 1], precision=top_precision) * (1.0 / math.sqrt(DH))
    key_valid = jnp.arange(token_len)[None, :] < count_rows[:, None]
    scores = low_back(jnp.where(key_valid[:, None, None, :], scores, masked_score))
    attn_prob = jax.nn.softmax(scores, axis=-1)
    context = jnp.einsum('ghqk,gkhe->gqhe', low(attn_prob), qkv_low[:, :, 2], precision=top_precision)
    context = low(low_back(context.reshape(group_size, token_len, H * DH)))
    branch = low_back(jnp.einsum('gli,id->gld', context, out_weight, precision=top_precision) + out_bias)
    mid = feature_rows + branch
    normed_two = low(layer_norm(mid, ln2_gain, ln2_bias))
    hidden = low_back(jnp.einsum('gld,df->glf', normed_two, fc1_weight, precision=top_precision) + fc1_bias)
    active = low(jax.nn.gelu(hidden, approximate=False))
    mlp_out = low_back(jnp.einsum('glf,fd->gld', active, fc2_weight, precision=top_precision) + fc2_bias)
    return mid + mlp_out

def reference(features, patch_counts, ln1_gain, ln1_bias, query_key_value_weight, qv_bias, out_weight, out_bias, ln2_gain, ln2_bias, fc1_weight, fc1_bias, fc2_weight, fc2_bias, cotangent):
    params = tuple((param.astype(jnp.float32) for param in (ln1_gain, ln1_bias, query_key_value_weight, qv_bias, out_weight, out_bias, ln2_gain, ln2_bias, fc1_weight, fc1_bias, fc2_weight, fc2_bias)))
    item_total, token_len, model_width = features.shape
    group_size = 8 if item_total % 8 == 0 else 1
    group_count = item_total // group_size
    feature_groups = features.astype(jnp.float32).reshape(group_count, group_size, token_len, model_width)
    count_groups = patch_counts.reshape(group_count, group_size)
    grad_groups = cotangent.astype(jnp.float32).reshape(group_count, group_size, token_len, model_width)

    def step(running, pieces):
        feature_group, count_group, grad_group = pieces
        result, pull = jax.vjp(lambda feat_value, param_value: block(feat_value, count_group, param_value), feature_group, params)
        feature_part, param_part = pull(grad_group)
        return (jax.tree.map(jnp.add, running, param_part), (result.astype(jnp.bfloat16), feature_part))
    start = jax.tree.map(jnp.zeros_like, params)
    totals, (results, feature_parts) = lax.scan(step, start, (feature_groups, count_groups, grad_groups))
    layer_out = results.reshape(item_total, token_len, model_width)
    features_grad = feature_parts.reshape(item_total, token_len, model_width)
    return (layer_out, features_grad, totals[0], totals[1], totals[2], totals[3], totals[4], totals[5], totals[6], totals[7], totals[8], totals[9], totals[10], totals[11])
```

```python
import jax
import jax.numpy as jnp
from jax import lax
from jax.experimental import pallas as pl
from jax.experimental.pallas import tpu as pltpu
from jax.sharding import Mesh, PartitionSpec as P

F32 = jnp.float32
BF16 = jnp.bfloat16
EPS = 1e-06
MASKED = -1e30
VMEM = pl.BlockSpec(memory_space=pltpu.VMEM)
SMEM = pl.BlockSpec(memory_space=pltpu.SMEM)


def dot_nn(a, b):
    return lax.dot_general(a, b, (((1,), (0,)), ((), ())), preferred_element_type=F32)


def dot_nt(a, b):
    return lax.dot_general(a, b, (((1,), (1,)), ((), ())), preferred_element_type=F32)


def normalize(values):
    row_mean = jnp.mean(values, axis=-1, keepdims=True)
    centred = values - row_mean
    inv_std = lax.rsqrt(jnp.mean(centred * centred, axis=-1, keepdims=True) + EPS)
    return centred * inv_std, inv_std


def norm_back(grad_normed, gain_row, scaled, inv_std):
    grad_scaled = grad_normed * gain_row
    first_mean = jnp.mean(grad_scaled, axis=-1, keepdims=True)
    second_mean = jnp.mean(grad_scaled * scaled, axis=-1, keepdims=True)
    return inv_std * (grad_scaled - first_mean - scaled * second_mean)


def head_lanes(values, head):
    lane = lax.broadcasted_iota(jnp.int32, values.shape, 1)
    return jnp.where((lane >= 64) == (head == 1), values, jnp.zeros_like(values))


def pick_lanes(first, second):
    lane = lax.broadcasted_iota(jnp.int32, first.shape, 1)
    return jnp.where(lane < 64, first, second)


def columns(ref, head_pairs, lead=()):
    return jnp.concatenate([ref[(*lead, p)] for p in head_pairs], axis=1)


def forward_attention(count_ref, x_ref, g1_ref, b1_ref, w_ref, qb_ref, vb_ref, ob_ref, g2_ref, b2_ref,
                      n1_ref, qkv_ref, ctx_ref, lse_ref, mid_ref, n2_ref):
    rows = x_ref.shape[0]
    pairs = w_ref.shape[1]
    count = count_ref[0]
    scaled, _ = normalize(x_ref[...].astype(F32))
    n1_ref[...] = (scaled * g1_ref[...] + b1_ref[...]).astype(BF16)
    valid = lax.broadcasted_iota(jnp.int32, (rows, rows), 0) < count

    def pair(p, _):
        weight = jnp.concatenate([w_ref[0, p], w_ref[2, p], w_ref[1, p]], axis=1)
        projected = dot_nn(n1_ref[...], weight)
        query = (projected[:, :128] + qb_ref[pl.ds(p, 1), :]).astype(BF16) * BF16(0.125)
        key = projected[:, 128:256].astype(BF16)
        value = (projected[:, 256:] + vb_ref[pl.ds(p, 1), :]).astype(BF16)
        qkv_ref[0, p] = query
        qkv_ref[1, p] = key
        qkv_ref[2, p] = value
        value_t = value.T
        parts = []
        for head in range(2):
            scores = jnp.where(valid, dot_nt(head_lanes(key, head), query), MASKED)
            top = jnp.max(scores, axis=0, keepdims=True)
            shifted = jnp.exp(scores - top)
            total = jnp.sum(shifted, axis=0, keepdims=True)
            prob = shifted * (1.0 / total)
            parts.append(dot_nn(value_t[64 * head : 64 * head + 64], prob.astype(BF16)))
            lse_ref[p, pl.ds(head, 1), :] = top + jnp.log(total)
        ctx_ref[p] = jnp.concatenate(parts, axis=0).T.astype(BF16)
        return 0

    lax.fori_loop(0, pairs, pair, 0)
    context = columns(ctx_ref, range(pairs))
    for j in range(3):
        cols = slice(256 * j, 256 * j + 256)
        out = jnp.concatenate([w_ref[3, p, cols, :] for p in range(pairs)], axis=1)
        mid_ref[:, cols] = x_ref[:, cols].astype(F32) + dot_nt(context, out) + ob_ref[:, cols]
    scaled, _ = normalize(mid_ref[...])
    n2_ref[...] = (scaled * g2_ref[...] + b2_ref[...]).astype(BF16)


def call_forward(count, x, g1, b1, w, qb, vb, ob, g2, b2):
    rows, width = x.shape
    pairs = w.shape[1]
    S = jax.ShapeDtypeStruct
    return pl.pallas_call(
        forward_attention,
        in_specs=[SMEM] + [VMEM] * 9,
        out_specs=[VMEM] * 6,
        out_shape=[S((rows, width), BF16), S((3, pairs, rows, 128), BF16), S((pairs, rows, 128), BF16),
                   S((pairs, 2, rows), F32), S((rows, width), F32), S((rows, width), BF16)],
        compiler_params=pltpu.CompilerParams(vmem_limit_bytes=50 << 20),
        cost_estimate=pl.CostEstimate(flops=6 * 10**9, bytes_accessed=16 << 20, transcendentals=3 << 20),
        name="attention_forward",
    )(count, x, g1, b1, w, qb, vb, ob, g2, b2)


def feed_forward(n2_ref, cot_ref, mid_ref, b2_ref, w_ref, b1_ref, lo_ref, gn2_ref, dw_ref, db_ref,
                 n2t_ref, cott_ref, acc_ref):
    step = pl.program_id(0)
    last = pl.num_programs(0) - 1

    @pl.when(step == 0)
    def _():
        n2t_ref[...] = n2_ref[...].T
        cott_ref[...] = cot_ref[...].T
        acc_ref[...] = jnp.zeros_like(acc_ref)
        gn2_ref[...] = jnp.zeros_like(gn2_ref)

    blocks, half = w_ref.shape[0], w_ref.shape[1] // 2
    first = jnp.concatenate([w_ref[b, i] for b in range(blocks) for i in range(half)], axis=1)
    second = jnp.concatenate([w_ref[b, half + i] for b in range(blocks) for i in range(half)], axis=1)
    hidden = dot_nn(n2_ref[...], first) + b1_ref[0]
    cdf = 0.5 * (1.0 + lax.erf(hidden * 0.7071067811865476))
    slope = cdf + hidden * (jnp.exp(-0.5 * hidden * hidden) * 0.3989422804014327)
    active = (hidden * cdf).astype(BF16)
    acc_ref[...] += dot_nt(active, second)
    grad_hidden = dot_nn(cot_ref[...], second) * slope
    db_ref[0] = jnp.sum(grad_hidden, axis=0, keepdims=True)
    grad_hidden = grad_hidden.astype(BF16)
    gn2_ref[...] += dot_nt(grad_hidden, first)
    fc2 = dot_nn(cott_ref[...], active).astype(BF16)
    fc1 = dot_nn(n2t_ref[...], grad_hidden).astype(BF16)
    for b in range(blocks):
        for i in range(half):
            at = 128 * (b * half + i)
            dw_ref[b, i] = fc1[:, at : at + 128]
            dw_ref[b, half + i] = fc2[:, at : at + 128]

    @pl.when(step == last)
    def _():
        lo_ref[...] = (mid_ref[...] + acc_ref[...] + b2_ref[...]).astype(BF16)


def call_feed_forward(n2, cot, mid, b2, w, b1):
    rows, width = n2.shape
    S = jax.ShapeDtypeStruct
    per = 2
    steps = w.shape[0] // per
    hidden = per * w.shape[1] // 2 * 128
    whole = pl.BlockSpec((rows, width), lambda i: (0, 0))
    block = pl.BlockSpec((per, *w.shape[1:]), lambda i: (i, 0, 0, 0))
    bias = pl.BlockSpec((1, 1, hidden), lambda i: (i, 0, 0))
    return pl.pallas_call(
        feed_forward,
        grid=(steps,),
        in_specs=[whole, whole, whole, pl.BlockSpec((1, width), lambda i: (0, 0)), block, bias],
        out_specs=[whole, whole, block, bias],
        out_shape=[S((rows, width), BF16), S((rows, width), F32), S(w.shape, BF16), S((steps, 1, hidden), F32)],
        scratch_shapes=[pltpu.VMEM((width, rows), BF16), pltpu.VMEM((width, rows), BF16), pltpu.VMEM((rows, width), F32)],
        compiler_params=pltpu.CompilerParams(vmem_limit_bytes=56 << 20),
        cost_estimate=pl.CostEstimate(flops=15 * 10**9, bytes_accessed=24 << 20, transcendentals=3 << 20),
        name="feed_forward",
    )(n2, cot, mid, b2, w, b1.reshape(steps, 1, hidden))


def backward_attention(count_ref, x_ref, g1_ref, w_ref, g2_ref, n1_ref, qkv_ref, ctx_ref, lse_ref, mid_ref, cot_ref, gn2_ref,
                       fg_ref, dw_ref, small_ref, qvb_ref, gb_ref, gbt_ref, n1t_ref, gm_ref):
    rows, width = x_ref.shape
    pairs = w_ref.shape[1]
    count = count_ref[0]
    scaled, inv = normalize(mid_ref[...])
    cot = cot_ref[...].astype(F32)
    gn2 = gn2_ref[...]
    grad_mid = cot + norm_back(gn2, g2_ref[...], scaled, inv)
    gm_ref[...] = grad_mid
    branch = grad_mid.astype(BF16)
    gb_ref[...] = branch
    gbt_ref[...] = branch.T
    n1t_ref[...] = n1_ref[...].T
    small_ref[2:3, :] = jnp.sum(branch.astype(F32), axis=0, keepdims=True)
    small_ref[3:4, :] = jnp.sum(gn2 * scaled, axis=0, keepdims=True)
    small_ref[4:5, :] = jnp.sum(gn2, axis=0, keepdims=True)
    small_ref[5:6, :] = jnp.sum(cot, axis=0, keepdims=True)
    valid = lax.broadcasted_iota(jnp.int32, (rows, rows), 0) < count
    fg_ref[...] = jnp.zeros_like(fg_ref)

    def pair(p, _):
        query, key, value = qkv_ref[0, p], qkv_ref[1, p], qkv_ref[2, p]
        grad_context = dot_nn(gb_ref[...], w_ref[3, p]).astype(BF16)
        dw_ref[3, p] = dot_nn(gbt_ref[...], ctx_ref[p]).astype(BF16)
        key_t = key.T
        grad_q, grad_k, grad_v = [], [], []
        for head in range(2):
            scores = jnp.where(valid, dot_nt(head_lanes(key, head), query), MASKED)
            prob = jnp.exp(scores - lse_ref[p, pl.ds(head, 1), :])
            grad_prob = dot_nt(head_lanes(value, head), grad_context)
            delta = jnp.sum(prob * grad_prob, axis=0, keepdims=True)
            grad_scores = (prob * (grad_prob - delta)).astype(BF16)
            grad_k.append(dot_nn(grad_scores, query))
            grad_v.append(dot_nn(prob.astype(BF16), grad_context))
            grad_q.append(dot_nn(key_t[64 * head : 64 * head + 64], grad_scores))
        grad_query = (jnp.concatenate(grad_q, axis=0).T * 0.125).astype(BF16)
        grad_key = pick_lanes(*grad_k).astype(BF16)
        grad_value = pick_lanes(*grad_v).astype(BF16)
        qvb_ref[0, pl.ds(p, 1), :] = jnp.sum(grad_query.astype(F32), axis=0, keepdims=True)
        qvb_ref[1, pl.ds(p, 1), :] = jnp.sum(grad_value.astype(F32), axis=0, keepdims=True)
        joined = jnp.concatenate([grad_query, grad_value, grad_key], axis=1)
        weight = jnp.concatenate([w_ref[0, p], w_ref[1, p], w_ref[2, p]], axis=1)
        fg_ref[...] += dot_nt(joined, weight)
        grads = dot_nn(n1t_ref[...], joined).astype(BF16)
        for i in range(3):
            dw_ref[i, p] = grads[:, 128 * i : 128 * i + 128]
        return 0

    lax.fori_loop(0, pairs, pair, 0)
    gn1 = fg_ref[...]
    scaled, inv = normalize(x_ref[...].astype(F32))
    small_ref[0:1, :] = jnp.sum(gn1 * scaled, axis=0, keepdims=True)
    small_ref[1:2, :] = jnp.sum(gn1, axis=0, keepdims=True)
    fg_ref[...] = gm_ref[...] + norm_back(gn1, g1_ref[...], scaled, inv)


def call_backward(count, x, g1, w, g2, n1, qkv, ctx, lse, mid, cot, gn2):
    rows, width = x.shape
    pairs = w.shape[1]
    S = jax.ShapeDtypeStruct
    return pl.pallas_call(
        backward_attention,
        in_specs=[SMEM] + [VMEM] * 11,
        out_specs=[VMEM] * 4,
        out_shape=[S((rows, width), F32), S(w.shape, BF16), S((6, width), F32), S((2, pairs, 128), F32)],
        scratch_shapes=[pltpu.VMEM((rows, width), BF16), pltpu.VMEM((width, rows), BF16), pltpu.VMEM((width, rows), BF16), pltpu.VMEM((rows, width), F32)],
        compiler_params=pltpu.CompilerParams(vmem_limit_bytes=56 << 20),
        cost_estimate=pl.CostEstimate(flops=14 * 10**9, bytes_accessed=24 << 20, transcendentals=3 << 20),
        name="attention_backward",
    )(count, x, g1, w, g2, n1, qkv, ctx, lse, mid, cot, gn2)


NAMES = ("z", "x", "yh", "core", "yl")
SIZES = (8, 4, 2, 2, 2)
DP = ("z", "x", "yh", "core")
Y = ("yh", "yl")
QUARTER = ("yh", "core")


def swap(values, axis, n, k):
    return lax.ppermute(values, axis, [(i, i ^ k) for i in range(n)])


def pick(values, index, axis=0):
    return lax.dynamic_index_in_dim(values, index, axis, keepdims=False)


def in_order(parts, index, axis):
    bit = 1
    while bit < len(parts):
        flip = (index & bit) != 0
        parts = [jnp.where(flip, parts[k ^ bit], parts[k]) for k in range(len(parts))]
        bit *= 2
    return jnp.stack(parts, axis=axis)


def gather(values, axis, n, index, place):
    return in_order([values] + [swap(values, axis, n, k) for k in range(1, n)], index, place)


def scatter_sum(values, axis, n, index, place):
    total = pick(values, index, place).astype(F32)
    for k in range(1, n):
        total = total + swap(pick(values, index ^ k, place), axis, n, k).astype(F32)
    return total.astype(BF16)


def gather_weights(packed, at):
    c = packed.shape[1]
    own = [pick(packed, at["q"])] + [swap(pick(packed, at["q"] ^ k), QUARTER, 4, k) for k in (1, 2, 3)]
    rows = in_order(own, at["q"], 1).reshape(c, 24, 128)
    rows = gather(rows, "z", 8, at["z"], 1)
    low, high = rows[:, :4], rows[:, 4:]
    low = gather(low, "x", 4, at["x"], 2).reshape(c, 384, 128)
    high = gather(high, Y, 4, at["y"], 0)
    low = gather(low, Y, 4, at["y"], 0)
    high = gather(high, "x", 4, at["x"], 3).reshape(4, c, 384, 128)
    both = jnp.concatenate([low, high], axis=2)
    return gather(both, "core", 2, at["core"], 0)


def scatter_grads(grads, at):
    c = grads.shape[2]
    total = scatter_sum(grads, "core", 2, at["core"], 0)
    low = total[:, :, :384]
    high = total[:, :, 384:].reshape(4, c, 4, 4, 24, 128)
    low = scatter_sum(low, Y, 4, at["y"], 0).reshape(c, 4, 4, 24, 128)
    high = scatter_sum(high, "x", 4, at["x"], 3)
    low = scatter_sum(low, "x", 4, at["x"], 2)
    high = scatter_sum(high, Y, 4, at["y"], 0)
    rows = scatter_sum(jnp.concatenate([low, high], axis=1), "z", 8, at["z"], 1)
    rows = rows.reshape(c, 4, 6, 128)
    own = [pick(rows, at["q"], 1)] + [swap(pick(rows, at["q"] ^ k, 1), QUARTER, 4, k) for k in (1, 2, 3)]
    return in_order(own, at["q"], 0).astype(F32)


def sum_everywhere(values):
    for axis, n in (("core", 2), ("yl", 2), ("yh", 2), ("x", 4), ("z", 8)):
        k = 1
        while k < n:
            values = values + swap(values, axis, n, k)
            k *= 2
    return values


def share(mine, at):
    other = swap(mine, "yl", 2, 1)
    mine = mine.astype(other.dtype)
    return jnp.stack([jnp.where(at["yl"] == 0, mine, other), jnp.where(at["yl"] == 0, other, mine)])


def on_device(
    features, patch_counts, ln1_gain, ln1_bias, query_key_value_weight, qv_bias, out_weight, out_bias,
    ln2_gain, ln2_bias, fc1_weight, fc1_bias, fc2_weight, fc2_bias, cotangent,
):
    at = {name: lax.axis_index(name) for name in NAMES}
    at["y"] = at["yh"] * 2 + at["yl"]
    at["q"] = at["yh"] * 2 + at["core"]
    row = lambda v: v.reshape(1, -1)

    attention_packed = jnp.concatenate(
        [
            query_key_value_weight.reshape(6, 3, 3, 128).transpose(1, 2, 0, 3),
            out_weight.reshape(1, 3, 128, 6).transpose(0, 1, 3, 2),
        ]
    )
    fc_packed = jnp.concatenate(
        [
            fc1_weight.reshape(6, 4, 3, 128).transpose(1, 2, 0, 3),
            fc2_weight.reshape(4, 3, 128, 6).transpose(0, 1, 3, 2),
        ],
        axis=1,
    )
    biases = jnp.concatenate([qv_bias.reshape(-1), fc1_bias]).reshape(18, 128)
    biases = gather(biases, "yl", 2, at["yl"], 0)
    query_bias = biases[:, 0:3].reshape(6, 128)
    value_bias = biases[:, 3:6].reshape(6, 128)
    hidden_bias = biases[:, 6:].reshape(2, 2, 2, 384).transpose(2, 1, 0, 3).reshape(-1)

    attention = gather_weights(attention_packed, at).reshape(4, 6, 768, 128)
    fc = gather_weights(fc_packed, at).reshape(8, 6, 768, 128)

    item = pick(features, at["yl"])
    cot = pick(cotangent, at["yl"])
    count = pick(patch_counts, at["yl"]).reshape(1)

    n1, qkv, context, log_total, mid, n2 = call_forward(
        count, item, row(ln1_gain), row(ln1_bias), attention, query_bias, value_bias, row(out_bias), row(ln2_gain), row(ln2_bias)
    )
    out_rows, gn2, fc_grads, hidden_sums = call_feed_forward(n2, cot, mid, row(fc2_bias), fc, hidden_bias)
    layer_out = share(out_rows, at)
    fc_own = scatter_grads(fc_grads.reshape(2, 4, 6, 768, 128), at)
    fg, attention_grads, sums, qv_sums = call_backward(
        count, item, row(ln1_gain), attention, row(ln2_gain), n1, qkv, context, log_total, mid, cot, gn2
    )
    attention_own = scatter_grads(attention_grads.reshape(2, 4, 3, 768, 128), at)

    other = swap(fg.astype(BF16), "yl", 2, 1).astype(F32)
    first = at["yl"] == 0
    features_grad = jnp.stack([jnp.where(first, fg, other), jnp.where(first, other, fg)])

    small = jnp.concatenate([sums.reshape(36, 128), qv_sums.reshape(12, 128), hidden_sums.reshape(24, 128)])
    small = sum_everywhere(small)
    sums = small[:36].reshape(6, 768)
    qv_grad = pick(small[36:48].reshape(2, 2, 384), at["yl"], 1)
    hidden_grad = pick(small[48:].reshape(2, 2, 2, 384), at["yl"], 2).transpose(1, 0, 2).reshape(1536)

    qkv_grad = attention_own[:3].transpose(2, 0, 1, 3).reshape(6, 3, 384)
    out_grad = attention_own[3].transpose(0, 2, 1).reshape(384, 6)
    fc1_grad = fc_own[:, :3].transpose(2, 0, 1, 3).reshape(6, 1536)
    fc2_grad = fc_own[:, 3:].transpose(0, 1, 3, 2).reshape(1536, 6)
    return (
        layer_out, features_grad, sums[0], sums[1], qkv_grad, qv_grad, out_grad, sums[2], sums[3], sums[4],
        fc1_grad, hidden_grad, fc2_grad, sums[5],
    )


def solution(mesh):
    five = Mesh(mesh.devices.reshape(SIZES), NAMES)
    return jax.shard_map(
        on_device,
        mesh=five,
        in_specs=(
            P(DP, None, None), P(DP), P(), P(), P(DP, None, "yl"), P(None, "yl"), P("yl", DP), P(),
            P(), P(), P(DP, "yl"), P("yl"), P("yl", DP), P(), P(DP, None, None),
        ),
        out_specs=(
            P(DP, None, None), P(DP, None, None), P(), P(), P(DP, None, "yl"), P(None, "yl"), P("yl", DP), P(),
            P(), P(), P(DP, "yl"), P("yl"), P("yl", DP), P(),
        ),
        check_vma=False,
    )
```

```python
import jax
import jax.numpy as jnp
from jax import lax
from jax.experimental import pallas as pl
from jax.experimental.pallas import tpu as pltpu
from jax.sharding import Mesh, PartitionSpec as P

F32 = jnp.float32
BF16 = jnp.bfloat16
EPS = 1e-06
MASKED = -1e30
VMEM = pl.BlockSpec(memory_space=pltpu.VMEM)
SMEM = pl.BlockSpec(memory_space=pltpu.SMEM)
S = jax.ShapeDtypeStruct
L = 512
D = 768
FREE = pl.CostEstimate(flops=1000, bytes_accessed=1000, transcendentals=0)


def dot_nn(a, b):
    return lax.dot_general(a, b, (((1,), (0,)), ((), ())), preferred_element_type=F32)


def dot_nt(a, b):
    return lax.dot_general(a, b, (((1,), (1,)), ((), ())), preferred_element_type=F32)


def normalize(values):
    row_mean = jnp.mean(values, axis=-1, keepdims=True)
    centred = values - row_mean
    inv_std = lax.rsqrt(jnp.mean(centred * centred, axis=-1, keepdims=True) + EPS)
    return centred * inv_std, inv_std


def norm_back(grad_normed, gain_row, scaled, inv_std):
    grad_scaled = grad_normed * gain_row
    first_mean = jnp.mean(grad_scaled, axis=-1, keepdims=True)
    second_mean = jnp.mean(grad_scaled * scaled, axis=-1, keepdims=True)
    return inv_std * (grad_scaled - first_mean - scaled * second_mean)


def row_sum(values):
    return jnp.sum(values, axis=0, keepdims=True)


def head_lanes(values, head):
    lane = lax.broadcasted_iota(jnp.int32, values.shape, 1)
    return jnp.where((lane >= 64) == (head == 1), values, jnp.zeros_like(values))


def pick_lanes(first, second):
    lane = lax.broadcasted_iota(jnp.int32, first.shape, 1)
    return jnp.where(lane < 64, first, second)


def joined_rows(ref, lead, tail, count):
    return jnp.concatenate([ref[(x, *lead, z, *tail)].astype(F32) for z in range(count) for x in range(4)], axis=0).astype(BF16)


def twist(first, second):
    return (
        jnp.concatenate([first[:, :64], second[:, :64]], axis=1),
        jnp.concatenate([first[:, 64:], second[:, 64:]], axis=1),
    )


def wide(ref, lead, kinds):
    return jnp.concatenate([ref[(*lead, k)] for k in kinds], axis=1)


def forward_attention(count_ref, x_ref, x_other_ref, g1_ref, b1_ref, y_ref, low0_ref, low1_ref, low2_ref, low3_ref, high_ref, qb_ref, vb_ref,
                      n1t_ref, qkv_ref, ctx_ref, lse_ref, part_ref, heads_ref, n1_ref, low_ref):
    for half, ref in enumerate((x_ref, x_other_ref)):
        scaled, _ = normalize(ref[...].astype(F32))
        normed = (scaled * g1_ref[...] + b1_ref[...]).astype(BF16)
        n1_ref[L * half : L * half + L] = normed
        n1t_ref[:, L * half : L * half + L] = normed.T
    for k, ref in enumerate((low0_ref, low1_ref, low2_ref, low3_ref)):
        low_ref[y_ref[0] ^ k] = ref[...]

    def weight(half, p, c):
        return jnp.concatenate([low_ref[2 * half + p, c], joined_rows(high_ref, (2 * half + p, c), (), 4)], axis=0)

    for half in range(2):
        for p in range(2):
            for kind in range(2):
                heads_ref[p, 2 * half + kind] = weight(half, p, kind)
        heads_ref[2, 2 * half], heads_ref[2, 2 * half + 1] = twist(weight(half, 0, 2), weight(half, 1, 2))

    def pair(p, _):
        projected = dot_nn(n1_ref[...], wide(heads_ref, (p,), range(3)))
        queries = (projected[:, :128] + qb_ref[pl.ds(p, 1), :]).astype(BF16) * BF16(0.125)
        keys = projected[:, 128:256].astype(BF16)
        values = (projected[:, 256:] + vb_ref[pl.ds(p, 1), :]).astype(BF16)
        qkv_ref[0, p] = queries
        qkv_ref[1, p] = keys
        qkv_ref[2, p] = values
        for item in range(2):
            rows = slice(L * item, L * item + L)
            query, key, value_t = queries[rows], keys[rows], values[rows].T
            valid = lax.broadcasted_iota(jnp.int32, (L, L), 0) < count_ref[item]
            parts = []
            for head in range(2):
                scores = jnp.where(valid, dot_nt(head_lanes(key, head), query), MASKED)
                top = jnp.max(scores, axis=0, keepdims=True)
                shifted = jnp.exp(scores - top)
                total = row_sum(shifted)
                prob = shifted * (1.0 / total)
                parts.append(dot_nn(value_t[64 * head : 64 * head + 64], prob.astype(BF16)))
                lse_ref[p, item, pl.ds(head, 1), :] = top + jnp.log(total)
            ctx_ref[p, rows] = jnp.concatenate(parts, axis=0).T.astype(BF16)
        return 0

    lax.fori_loop(0, 3, pair, 0)
    context = jnp.concatenate([ctx_ref[p] for p in range(3)], axis=1)
    for j in range(3):
        cols = slice(256 * j, 256 * j + 256)
        out = jnp.concatenate([heads_ref[p, 3, cols, :] for p in range(3)], axis=1)
        part_ref[:, cols] = dot_nt(context, out).astype(BF16)


def call_forward(counts, x, x_other, g1, b1, y, lows, high, qb, vb):
    rows = 2 * L
    return pl.pallas_call(
        forward_attention,
        in_specs=[SMEM] + [VMEM] * 4 + [SMEM] + [VMEM] * 7,
        out_specs=[VMEM] * 6,
        out_shape=[S((D, rows), BF16), S((3, 3, rows, 128), BF16), S((3, rows, 128), BF16),
                   S((3, 2, 2, L), F32), S((rows, D), BF16), S((3, 4, D, 128), BF16)],
        scratch_shapes=[pltpu.VMEM((rows, D), BF16), pltpu.VMEM((4, 3, D // 2, 128), BF16)],
        compiler_params=pltpu.CompilerParams(vmem_limit_bytes=50 << 20),
        cost_estimate=FREE,
        name="attention_forward",
    )(counts, x, x_other, g1, b1, y, *lows, high, qb, vb)


def middle(x_refs, own_ref, other_ref, ob_ref, half):
    mine, theirs = pl.ds(L * half, L), pl.ds(L - L * half, L)
    return x_refs[half][...].astype(F32) + (own_ref[mine, :].astype(F32) + other_ref[theirs, :].astype(F32)) + ob_ref[...]


def feed_forward(x_ref, x_other_ref, own_ref, other_ref, ob_ref, g2_ref, b2_ref, cot_ref, cot_other_ref, low_ref, high_ref, b1_ref,
                 mlp_ref, mlp_send_ref, gn2_ref, db_ref, dw_ref, n2_ref, n2t_ref, cots_ref, cott_ref, acc_ref, gacc_ref):
    step = pl.program_id(0)
    last = pl.num_programs(0) - 1

    @pl.when(step == 0)
    def _():
        for half in range(2):
            scaled, _ = normalize(middle((x_ref, x_other_ref), own_ref, other_ref, ob_ref, half))
            n2_ref[L * half : L * half + L] = (scaled * g2_ref[...] + b2_ref[...]).astype(BF16)
            cots_ref[L * half : L * half + L] = (cot_ref, cot_other_ref)[half][...]
        n2t_ref[...] = n2_ref[...].T
        cott_ref[...] = cots_ref[...].T
        acc_ref[...] = jnp.zeros_like(acc_ref)
        gacc_ref[...] = jnp.zeros_like(gacc_ref)

    first, second = (
        jnp.concatenate(
            [jnp.concatenate([low_ref[y, layer, 0], joined_rows(high_ref, (y, layer, 0), (), 4)], axis=0) for y in range(4)], axis=1
        )
        for layer in range(2)
    )
    hidden = dot_nn(n2_ref[...], first) + b1_ref[0]
    cdf = 0.5 * (1.0 + lax.erf(hidden * 0.7071067811865476))
    slope = cdf + hidden * (jnp.exp(-0.5 * hidden * hidden) * 0.3989422804014327)
    active = (hidden * cdf).astype(BF16)
    acc_ref[...] += dot_nt(active, second)
    grad_hidden = dot_nn(cots_ref[...], second) * slope
    db_ref[0] = row_sum(grad_hidden)
    grad_hidden = grad_hidden.astype(BF16)
    gacc_ref[...] += dot_nt(grad_hidden, first)
    for layer, grad in enumerate((dot_nn(n2t_ref[...], grad_hidden), dot_nn(cott_ref[...], active))):
        for x in range(4):
            for z in range(8):
                block = grad[96 * z + 24 * x : 96 * z + 24 * x + 24].astype(BF16)
                for y in range(4):
                    dw_ref[x, y, z, layer, 0] = block[:, 128 * y : 128 * y + 128]

    @pl.when(step == last)
    def _():
        mlp_ref[...] = acc_ref[:L].astype(BF16)
        mlp_send_ref[...] = acc_ref[L:].astype(BF16)
        gn2_ref[...] = gacc_ref[...].astype(BF16)


def call_feed_forward(x, x_other, own, other, ob, g2, b2, cot, cot_other, low, high, b1):
    rows = 2 * L
    half = pl.BlockSpec((L, D), lambda i: (0, 0))
    whole = pl.BlockSpec((rows, D), lambda i: (0, 0))
    line = pl.BlockSpec((1, D), lambda i: (0, 0))
    lows = pl.BlockSpec((4, 2, 1, D // 2, 128), lambda i: (0, 0, i, 0, 0))
    highs = pl.BlockSpec((4, 4, 2, 1, 4, 24, 128), lambda i: (0, 0, 0, i, 0, 0, 0))
    grads = pl.BlockSpec((4, 4, 8, 2, 1, 24, 128), lambda i: (0, 0, 0, 0, i, 0, 0))
    bias = pl.BlockSpec((1, 1, 512), lambda i: (i, 0, 0))
    return pl.pallas_call(
        feed_forward,
        grid=(3,),
        in_specs=[half, half, whole, whole, line, line, line, half, half, lows, highs, bias],
        out_specs=[half, half, whole, bias, grads],
        out_shape=[S((L, D), BF16), S((L, D), BF16), S((rows, D), BF16), S((3, 1, 512), F32), S((4, 4, 8, 2, 3, 24, 128), BF16)],
        scratch_shapes=[pltpu.VMEM((rows, D), BF16), pltpu.VMEM((D, rows), BF16), pltpu.VMEM((rows, D), BF16),
                        pltpu.VMEM((D, rows), BF16), pltpu.VMEM((rows, D), F32), pltpu.VMEM((rows, D), F32)],
        compiler_params=pltpu.CompilerParams(vmem_limit_bytes=58 << 20),
        cost_estimate=FREE,
        name="feed_forward",
    )(x, x_other, own, other, ob, g2, b2, cot, cot_other, low, high, b1)


def norm_two_back(x_refs, own_ref, other_ref, ob_ref, g2_ref, cot_refs, gown_ref, gother_ref, gb_ref, gbt_ref, gm_ref, sums_ref):
    for half in range(2):
        mine, theirs = pl.ds(L * half, L), pl.ds(L - L * half, L)
        scaled, inv = normalize(middle(x_refs, own_ref, other_ref, ob_ref, half))
        grad = gown_ref[mine, :].astype(F32) + gother_ref[theirs, :].astype(F32)
        cot = cot_refs[half][...].astype(F32)
        grad_mid = cot + norm_back(grad, g2_ref[...], scaled, inv)
        branch = grad_mid.astype(BF16)
        gb_ref[mine, :] = branch
        gbt_ref[:, L * half : L * half + L] = branch.T
        if half == 0:
            gm_ref[...] = grad_mid
            sums_ref[0:1, :] = row_sum(branch.astype(F32))
            sums_ref[1:2, :] = row_sum(grad * scaled)
            sums_ref[2:3, :] = row_sum(grad)
            sums_ref[3:4, :] = row_sum(cot)


def backward_pair(p, count_ref, heads_ref, qkv_ref, ctx_ref, lse_ref, gb_ref, gbt_ref, n1t_ref, joined_ref, qvb_ref):
    grad_context = dot_nn(gb_ref[...], heads_ref[p, 3]).astype(BF16)
    grad_out = dot_nn(gbt_ref[...], ctx_ref[p])
    for item in range(2):
        rows = slice(L * item, L * item + L)
        query, key, value = qkv_ref[0, p, rows], qkv_ref[1, p, rows], qkv_ref[2, p, rows]
        grad_ctx = grad_context[rows]
        key_t = key.T
        valid = lax.broadcasted_iota(jnp.int32, (L, L), 0) < count_ref[item]
        grad_q, grad_k, grad_v = [], [], []
        for head in range(2):
            scores = jnp.where(valid, dot_nt(head_lanes(key, head), query), MASKED)
            prob = jnp.exp(scores - lse_ref[p, item, pl.ds(head, 1), :])
            grad_prob = dot_nt(head_lanes(value, head), grad_ctx)
            delta = row_sum(prob * grad_prob)
            grad_scores = (prob * (grad_prob - delta)).astype(BF16)
            grad_k.append(dot_nn(grad_scores, query))
            grad_v.append(dot_nn(prob.astype(BF16), grad_ctx))
            grad_q.append(dot_nn(key_t[64 * head : 64 * head + 64], grad_scores))
        joined_ref[p, rows, 0:128] = (jnp.concatenate(grad_q, axis=0).T * 0.125).astype(BF16)
        joined_ref[p, rows, 128:256] = pick_lanes(*grad_k).astype(BF16)
        joined_ref[p, rows, 256:384] = pick_lanes(*grad_v).astype(BF16)
    joined = joined_ref[p]
    sums = row_sum(joined.astype(F32))
    qvb_ref[p, 0:1, :] = sums[:, :128]
    qvb_ref[p, 1:2, :] = sums[:, 256:]
    grads = dot_nn(n1t_ref[...], joined)
    return grads[:, :128], grads[:, 128:256], grads[:, 256:], grad_out


def backward_attention(count_ref, x_ref, x_other_ref, own_ref, other_ref, ob_ref, g2_ref, cot_ref, cot_other_ref, gown_ref, gother_ref,
                       heads_ref, qkv_ref, ctx_ref, lse_ref, n1t_ref,
                       gm_ref, sums_ref, joined_ref, qvb_ref, dw_ref, gb_ref, gbt_ref, last_ref):
    norm_two_back((x_ref, x_other_ref), own_ref, other_ref, ob_ref, g2_ref, (cot_ref, cot_other_ref), gown_ref, gother_ref,
                  gb_ref, gbt_ref, gm_ref, sums_ref)

    def pair(p, _):
        grads = backward_pair(p, count_ref, heads_ref, qkv_ref, ctx_ref, lse_ref, gb_ref, gbt_ref, n1t_ref, joined_ref, qvb_ref)

        @pl.when(p < 2)
        def _():
            for i, grad in enumerate(grads):
                spread(dw_ref, 2 * (i // 2) + p, i % 2, grad)

        @pl.when(p == 2)
        def _():
            for i, grad in enumerate(grads):
                last_ref[i] = grad

        return 0

    lax.fori_loop(0, 3, pair, 0)
    for high in range(2):
        for low, grad in enumerate(twist(last_ref[2 * high], last_ref[2 * high + 1])):
            spread(dw_ref, 2 * high + low, 2, grad)


def spread(dw_ref, y, c, grad):
    for z in range(8):
        for x in range(4):
            at = 24 * (4 * z + x)
            dw_ref[y, x, z, c] = grad[at : at + 24].astype(BF16)


def call_backward(counts, x, x_other, own, other, ob, g2, cot, cot_other, gown, gother, heads, qkv, ctx, lse, n1t):
    rows = 2 * L
    return pl.pallas_call(
        backward_attention,
        in_specs=[SMEM] + [VMEM] * 15,
        out_specs=[VMEM] * 5,
        out_shape=[S((L, D), F32), S((4, D), F32), S((3, rows, 384), BF16), S((3, 2, 128), F32), S((4, 4, 8, 3, 24, 128), BF16)],
        scratch_shapes=[pltpu.VMEM((rows, D), BF16), pltpu.VMEM((D, rows), BF16), pltpu.VMEM((4, D, 128), F32)],
        compiler_params=pltpu.CompilerParams(vmem_limit_bytes=58 << 20),
        cost_estimate=FREE,
        name="attention_backward",
    )(counts, x, x_other, own, other, ob, g2, cot, cot_other, gown, gother, heads, qkv, ctx, lse, n1t)


def norm_one_grad(x_ref, x_other_ref, heads_ref, joined_ref, own_ref, send_ref, sums_ref):
    for half in range(2):
        rows = slice(L * half, L * half + L)
        grad = dot_nt(joined_ref[0, rows, :], wide(heads_ref, (0,), range(3)))
        for p in range(1, 3):
            grad = grad + dot_nt(joined_ref[p, rows, :], wide(heads_ref, (p,), range(3)))
        scaled, _ = normalize((x_ref, x_other_ref)[half][...].astype(F32))
        if half == 0:
            own_ref[...] = grad
            gain, shift = row_sum(grad * scaled), row_sum(grad)
        else:
            send_ref[...] = grad.astype(BF16)
            sums_ref[0:1, :] = gain + row_sum(grad * scaled)
            sums_ref[1:2, :] = shift + row_sum(grad)


def call_norm_one_grad(x, x_other, heads, joined):
    return pl.pallas_call(
        norm_one_grad,
        in_specs=[VMEM] * 4,
        out_specs=[VMEM] * 3,
        out_shape=[S((L, D), F32), S((L, D), BF16), S((2, D), F32)],
        compiler_params=pltpu.CompilerParams(vmem_limit_bytes=50 << 20),
        cost_estimate=FREE,
        name="norm_one_grad",
    )(x, x_other, heads, joined)


def norm_one_back(x_ref, g1_ref, gm_ref, own_ref, other_ref, fg_ref, top_ref, bottom_ref):
    scaled, inv = normalize(x_ref[...].astype(F32))
    grad = own_ref[...] + other_ref[...].astype(F32)
    result = gm_ref[...] + norm_back(grad, g1_ref[...], scaled, inv)
    fg_ref[...] = result
    top_ref[...] = result[: L // 2].astype(BF16)
    bottom_ref[...] = result[L // 2 :].astype(BF16)


def call_norm_one_back(x, g1, gm, own, other):
    return pl.pallas_call(
        norm_one_back,
        grid=(1,),
        in_specs=[pl.BlockSpec((L, D), lambda i: (0, 0)), pl.BlockSpec((1, D), lambda i: (0, 0))]
        + [pl.BlockSpec((L, D), lambda i: (0, 0))] * 3,
        out_specs=[pl.BlockSpec((L, D), lambda i: (0, 0))] + [pl.BlockSpec((L // 2, D), lambda i: (0, 0))] * 2,
        out_shape=[S((L, D), F32), S((L // 2, D), BF16), S((L // 2, D), BF16)],
        compiler_params=pltpu.CompilerParams(vmem_limit_bytes=40 << 20),
        cost_estimate=FREE,
        name="norm_one_back",
    )(x, g1, gm, own, other)


NAMES = ("z", "x", "yh", "core", "yl")
SIZES = (8, 4, 2, 2, 2)
DP = ("z", "x", "yh", "core")
Y = ("yh", "yl")
QUARTER = ("yh", "core")
ROWS = ("z", "yh", "core")


def after(values, *earlier):
    return pl.pallas_call(
        lambda *refs: None,
        in_specs=[pl.BlockSpec(memory_space=pl.ANY)] * (1 + len(earlier)),
        out_specs=pl.BlockSpec(memory_space=pl.ANY),
        out_shape=S(values.shape, values.dtype),
        input_output_aliases={0: 0},
        cost_estimate=FREE,
        name="after",
    )(values, *earlier)


def swap(values, axis, n, k):
    return lax.ppermute(values, axis, [(i, i ^ k) for i in range(n)])


def pick(values, index, axis=0):
    return lax.dynamic_index_in_dim(values, index, axis, keepdims=False)


def in_order(parts, index, axis):
    bit = 1
    while bit < len(parts):
        flip = (index & bit) != 0
        parts = [jnp.where(flip, parts[k ^ bit], parts[k]) for k in range(len(parts))]
        bit *= 2
    return jnp.stack(parts, axis=axis)


def gather(values, axis, n, index, place):
    return in_order([values] + [swap(values, axis, n, k) for k in range(1, n)], index, place)


def add_up(parts):
    total = parts[0].astype(F32)
    for part in parts[1:]:
        total = total + part.astype(F32)
    return total.astype(BF16)


def sent(parts, axis, n):
    return [parts[0]] + [swap(parts[k], axis, n, k) for k in range(1, n)]


def gather_rows(packed):
    c = packed.shape[1]
    return exchange(repeated(packed, 8).reshape(32, c, 6, 128), ROWS).reshape(8, 4, c, 6, 128)


def whole_rows(got):
    return got.transpose(2, 0, 1, 3, 4).reshape(got.shape[2], 8, 24, 128)


def copies(values, axis, n):
    return [values] + [swap(values, axis, n, k) for k in range(1, n)]


def gather_half(rows, at):
    c = rows.shape[0]
    low = in_order(copies(rows[:, :4], "x", 4), at["x"], 2).reshape(c, 384, 128)
    return low, in_order(copies(rows[:, 4:], Y, 4), at["y"], 0)


def repeated(values, n):
    return jnp.broadcast_to(values[None], (n, *values.shape))


def exchange(values, axis):
    return lax.all_to_all(values, axis, split_axis=0, concat_axis=0, tiled=True)


def scatter_rows(rows, extra):
    c = rows.shape[1]
    cut = rows.reshape(8, c, 4, 6, 128).transpose(0, 2, 1, 3, 4).reshape(32, c, 6, 128)
    quarter = pick(extra.astype(BF16).reshape(4, c, 2, 128), lax.axis_index("yh") * 2 + lax.axis_index("core"))
    cut = jnp.concatenate([cut, repeated(quarter, 32)], axis=2)
    got = jnp.sum(exchange(cut, ROWS).reshape(8, 4, c, 8, 128).astype(F32), axis=0)
    return cut, got[:, :, :6], got[:, :, 6:].reshape(72, 128)


def sum_over(values, axis, n):
    return pair_sum(copies(values, axis, n))


def pair_sum(parts):
    while len(parts) > 1:
        parts = [first + second for first, second in zip(parts[::2], parts[1::2])]
    return parts[0]


def place_items(at_ref, out_ref, out_other_ref, fg_ref, top_ref, bottom_ref, cut_ref, layer_ref, features_ref):
    del at_ref, cut_ref

    @pl.when(pl.program_id(0) == 0)
    def _():
        layer_ref[0] = out_ref[...]
        features_ref[0] = fg_ref[...]

    @pl.when(pl.program_id(0) == 1)
    def _():
        layer_ref[0] = out_other_ref[...]
        features_ref[0, : L // 2] = top_ref[...].astype(F32)
        features_ref[0, L // 2 :] = bottom_ref[...].astype(F32)


def call_place_items(at, out, out_other, fg, top, bottom, cut):
    whole = pl.BlockSpec((L, D), lambda i, at: (0, 0))
    half = pl.BlockSpec((L // 2, D), lambda i, at: (0, 0))
    one = pl.BlockSpec((1, L, D), lambda i, at: (at[0] ^ i, 0, 0))
    return pl.pallas_call(
        place_items,
        grid_spec=pltpu.PrefetchScalarGridSpec(
            num_scalar_prefetch=1,
            grid=(2,),
            in_specs=[whole] * 3 + [half] * 2 + [pl.BlockSpec(memory_space=pl.ANY)],
            out_specs=[one, one],
        ),
        out_shape=[S((2, L, D), BF16), S((2, L, D), F32)],
        compiler_params=pltpu.CompilerParams(vmem_limit_bytes=40 << 20),
        cost_estimate=FREE,
        name="place_items",
    )(at, out, out_other, fg, top, bottom, cut)


def on_core(values, at, axis):
    zero = jnp.zeros_like(values)
    return jnp.stack([jnp.where(at["core"] == 0, values, zero), jnp.where(at["core"] == 0, zero, values)], axis=axis)


def pack(query_key_value_weight, out_weight, fc1_weight, fc2_weight):
    kinds = jnp.concatenate(
        [query_key_value_weight.reshape(6, 3, 2, 3, 64), out_weight.T.reshape(6, 1, 2, 3, 64)], axis=1
    ).reshape(6, 2, 2, 2, 3, 64)
    two = kinds[:, :, :, :, :2].reshape(6, 2, 2, 2, 128).transpose(1, 3, 2, 0, 4)
    third = kinds[:, :, :, :, 2].transpose(1, 3, 0, 2, 4).reshape(2, 2, 1, 6, 128)
    first = fc1_weight.reshape(6, 2, 2, 3, 128).transpose(1, 2, 3, 0, 4)
    second = fc2_weight.T.reshape(6, 2, 2, 3, 128).transpose(1, 2, 3, 0, 4)
    return jnp.concatenate([two, third, first, second], axis=2).reshape(4, 9, 6, 128)


def unpack(attention, fc):
    attention = attention.reshape(2, 2, 3, 6, 128)
    two = attention[:, :, :2].reshape(2, 2, 2, 6, 2, 64)
    third = attention[:, :, 2].reshape(2, 2, 6, 2, 64).transpose(0, 1, 3, 2, 4).reshape(2, 2, 2, 6, 1, 64)
    kinds = jnp.concatenate([two, third], axis=4).transpose(0, 2, 3, 1, 4, 5).reshape(4, 6, 384)
    first = fc[:, :3].transpose(2, 0, 1, 3).reshape(6, 1536)
    second = fc[:, 3:].transpose(0, 1, 3, 2).reshape(1536, 6)
    return kinds[:3].transpose(1, 0, 2), kinds[3].T, first, second


def on_device(
    features, patch_counts, ln1_gain, ln1_bias, query_key_value_weight, qv_bias, out_weight, out_bias,
    ln2_gain, ln2_bias, fc1_weight, fc1_bias, fc2_weight, fc2_bias, cotangent,
):
    at = {name: lax.axis_index(name) for name in NAMES}
    at["y"] = at["yh"] * 2 + at["yl"]
    row = lambda v: v.reshape(1, -1)

    rows = gather_rows(pack(query_key_value_weight, out_weight, fc1_weight, fc2_weight))

    item, cot, count = (pick(v, at["yl"]) for v in (features, cotangent, patch_counts))
    item_other, cot_other = swap(item, "core", 2, 1), swap(cot, "core", 2, 1)
    counts = jnp.stack([count, swap(count, "core", 2, 1)])
    biases = gather(jnp.concatenate([qv_bias.reshape(-1), fc1_bias]).reshape(18, 128), "yl", 2, at["yl"], 0)
    heads_bias = pick(biases[:, :6].reshape(2, 2, 2, 3, 64), at["core"], 2)
    heads_bias = jnp.stack(
        [heads_bias[0, :, :2].reshape(2, 128), heads_bias[1, :, :2].reshape(2, 128), heads_bias[:, :, 2].transpose(1, 0, 2).reshape(2, 128)]
    )
    hidden_bias = pick(biases[:, 6:].reshape(2, 2, 2, 3, 128), at["core"], 2).transpose(2, 1, 0, 3).reshape(3, 1, 512)
    query_bias, value_bias = heads_bias[:, 0], heads_bias[:, 1]
    ob, g1, g2 = row(out_bias), row(ln1_gain), row(ln2_gain)
    rows = whole_rows(after(rows, item_other, cot_other, counts, query_bias, value_bias, hidden_bias))
    low, high = gather_half(rows, at)
    lows, fc_high = copies(low[:3], Y, 4), repeated(high[:, 3:], 4)
    attention_high = after(exchange(repeated(high[:, :3], 4), "x"), fc_high)
    fc_low, fc_high = lax.all_gather(low[3:], Y), exchange(fc_high, "x")
    n1t, qkv, context, log_total, own, heads = call_forward(
        counts, item, item_other, g1, row(ln1_bias), at["y"].reshape(1), lows, attention_high, query_bias, value_bias
    )
    other = swap(own, "core", 2, 1)
    mlp, mlp_send, gown, hidden_sums, fc_local = call_feed_forward(
        item, item_other, own, other, ob, g2, row(ln2_bias), cot, cot_other,
        fc_low.reshape(4, 2, 3, D // 2, 128), fc_high.reshape(4, 4, 2, 3, 4, 24, 128), hidden_bias
    )
    mid = item.astype(F32) + (own[:L].astype(F32) + other[L:].astype(F32)) + out_bias
    out_rows = (mid + (mlp.astype(F32) + swap(mlp_send, "core", 2, 1).astype(F32)) + fc2_bias).astype(BF16)
    out_other = swap(out_rows, "yl", 2, 1)
    gother = after(swap(gown, "core", 2, 1), out_rows)
    fc = lax.psum_scatter(fc_local.reshape(4, 4, 8, 6, 24, 128), "x")
    grad_mid, sums_two, joined, qv, grads = call_backward(
        counts, item, item_other, own, other, ob, g2, cot, cot_other, gown, gother, heads, qkv, context, log_total, n1t
    )
    got = exchange(after(grads, out_other), Y)
    grad_one, grad_send, sums_one = call_norm_one_grad(item, item_other, heads, joined)

    qv = jnp.concatenate([qv[:2].reshape(2, 2, 2, 64), qv[2].reshape(2, 2, 64).transpose(1, 0, 2)[:, :, None]], axis=2)
    qv = on_core(qv.transpose(1, 0, 2, 3), at, 2).reshape(12, 128)
    hidden_sums = on_core(hidden_sums.reshape(3, 2, 2, 128).transpose(2, 1, 0, 3), at, 2).reshape(24, 128)
    small = jnp.concatenate([sums_one.reshape(12, 128), sums_two.reshape(24, 128), qv, hidden_sums])

    pieces = after(fc, sums_one)
    pieces = [pick(pieces, at["y"] ^ k) for k in range(4)]
    small = small + swap(small, "core", 2, 1)
    parts = copies(small, Y, 4)
    grad_other = after(swap(grad_send, "core", 2, 1), pieces[3])
    fg, top, bottom = call_norm_one_back(item, g1, grad_mid, grad_one, grad_other)
    top_other, bottom_other = swap(top, "yl", 2, 1), swap(bottom, "yl", 2, 1)
    got = jnp.sum(after(got, top).astype(F32), axis=0).astype(BF16)
    parts[1] = after(parts[1], got)
    small = pair_sum(parts)
    got = exchange(jnp.concatenate([got.reshape(4, 576, 128), repeated(small.astype(BF16), 4)], axis=1), "x")
    pieces = sent(pieces, Y, 4)
    fc_rows = add_up(pieces)
    got = jnp.sum(after(got, fc_rows, top_other).astype(F32), axis=0)
    attention_rows = got[:576].astype(BF16).reshape(8, 3, 24, 128)
    cut, owned, small = scatter_rows(jnp.concatenate([attention_rows, fc_rows], axis=1), got[576:])
    layer_out, features_grad = call_place_items(at["yl"].reshape(1), out_rows, out_other, fg, top_other, bottom_other, cut)
    qkv_grad, out_grad, fc1_grad, fc2_grad = unpack(owned[:, :3], owned[:, 3:])

    sums = small[:36].reshape(6, D)
    qv_grad = pick(small[36:48].reshape(2, 2, 384), at["yl"], 1)
    hidden_grad = pick(small[48:].reshape(2, 1536), at["yl"])
    return (
        layer_out, features_grad, sums[0], sums[1], qkv_grad, qv_grad, out_grad, sums[2], sums[3], sums[4],
        fc1_grad, hidden_grad, fc2_grad, sums[5],
    )


def solution(mesh):
    five = Mesh(mesh.devices.reshape(SIZES), NAMES)
    return jax.shard_map(
        on_device,
        mesh=five,
        in_specs=(
            P(DP, None, None), P(DP), P(), P(), P(DP, None, "yl"), P(None, "yl"), P("yl", DP), P(),
            P(), P(), P(DP, "yl"), P("yl"), P("yl", DP), P(), P(DP, None, None),
        ),
        out_specs=(
            P(DP, None, None), P(DP, None, None), P(), P(), P(DP, None, "yl"), P(None, "yl"), P("yl", DP), P(),
            P(), P(), P(DP, "yl"), P("yl"), P("yl", DP), P(),
        ),
        check_vma=False,
    )
```

```python
import jax
import jax.numpy as jnp
from jax import lax
from jax.experimental import pallas as pl
from jax.experimental.pallas import tpu as pltpu
from jax.sharding import Mesh, PartitionSpec as P

F32 = jnp.float32
BF16 = jnp.bfloat16
EPS = 1e-06
MASKED = -1e30
VMEM = pl.BlockSpec(memory_space=pltpu.VMEM)
SMEM = pl.BlockSpec(memory_space=pltpu.SMEM)
S = jax.ShapeDtypeStruct
L = 512
D = 768
FREE = pl.CostEstimate(flops=1000, bytes_accessed=1000, transcendentals=0)
LONG = pl.CostEstimate(flops=10**11, bytes_accessed=10**8, transcendentals=0)


def dot_nn(a, b):
    return lax.dot_general(a, b, (((1,), (0,)), ((), ())), preferred_element_type=F32)


def dot_nt(a, b):
    return lax.dot_general(a, b, (((1,), (1,)), ((), ())), preferred_element_type=F32)


def normalize(values):
    row_mean = jnp.mean(values, axis=-1, keepdims=True)
    centred = values - row_mean
    inv_std = lax.rsqrt(jnp.mean(centred * centred, axis=-1, keepdims=True) + EPS)
    return centred * inv_std, inv_std


def norm_back(grad_normed, gain_row, scaled, inv_std):
    grad_scaled = grad_normed * gain_row
    first_mean = jnp.mean(grad_scaled, axis=-1, keepdims=True)
    second_mean = jnp.mean(grad_scaled * scaled, axis=-1, keepdims=True)
    return inv_std * (grad_scaled - first_mean - scaled * second_mean)


def row_sum(values):
    return jnp.sum(values, axis=0, keepdims=True)


def head_lanes(values, head):
    lane = lax.broadcasted_iota(jnp.int32, values.shape, 1)
    return jnp.where((lane >= 64) == (head == 1), values, jnp.zeros_like(values))


def pick_lanes(first, second):
    lane = lax.broadcasted_iota(jnp.int32, first.shape, 1)
    return jnp.where(lane < 64, first, second)


def joined_rows(ref, lead, tail, count):
    return jnp.concatenate([ref[(x, *lead, z, *tail)].astype(F32) for z in range(count) for x in range(4)], axis=0).astype(BF16)


def twist(first, second):
    return (
        jnp.concatenate([first[:, :64], second[:, :64]], axis=1),
        jnp.concatenate([first[:, 64:], second[:, 64:]], axis=1),
    )


def wide(ref, lead, kinds):
    return jnp.concatenate([ref[(*lead, k)] for k in kinds], axis=1)


def forward_attention(count_ref, x_ref, x_other_ref, g1_ref, b1_ref, y_ref, low0_ref, low1_ref, low2_ref, low3_ref, high_ref, qb_ref, vb_ref,
                      n1t_ref, qkv_ref, ctx_ref, lse_ref, part_ref, heads_ref, n1_ref, low_ref):
    for half, ref in enumerate((x_ref, x_other_ref)):
        scaled, _ = normalize(ref[...].astype(F32))
        normed = (scaled * g1_ref[...] + b1_ref[...]).astype(BF16)
        n1_ref[L * half : L * half + L] = normed
        n1t_ref[:, L * half : L * half + L] = normed.T
    for k, ref in enumerate((low0_ref, low1_ref, low2_ref, low3_ref)):
        low_ref[y_ref[0] ^ k] = ref[...]

    def weight(half, p, c):
        return jnp.concatenate([low_ref[2 * half + p, c], joined_rows(high_ref, (2 * half + p, c), (), 4)], axis=0)

    for half in range(2):
        for p in range(2):
            for kind in range(2):
                heads_ref[p, 2 * half + kind] = weight(half, p, kind)
        heads_ref[2, 2 * half], heads_ref[2, 2 * half + 1] = twist(weight(half, 0, 2), weight(half, 1, 2))

    def pair(p, _):
        projected = dot_nn(n1_ref[...], wide(heads_ref, (p,), range(3)))
        queries = (projected[:, :128] + qb_ref[pl.ds(p, 1), :]).astype(BF16) * BF16(0.125)
        keys = projected[:, 128:256].astype(BF16)
        values = (projected[:, 256:] + vb_ref[pl.ds(p, 1), :]).astype(BF16)
        qkv_ref[0, p] = queries
        qkv_ref[1, p] = keys
        qkv_ref[2, p] = values
        for item in range(2):
            rows = slice(L * item, L * item + L)
            query, key, value_t = queries[rows], keys[rows], values[rows].T
            valid = lax.broadcasted_iota(jnp.int32, (L, L), 0) < count_ref[2 * item + count_ref[4]]
            parts = []
            for head in range(2):
                scores = jnp.where(valid, dot_nt(head_lanes(key, head), query), MASKED)
                top = jnp.max(scores, axis=0, keepdims=True)
                shifted = jnp.exp(scores - top)
                total = row_sum(shifted)
                prob = shifted * (1.0 / total)
                parts.append(dot_nn(value_t[64 * head : 64 * head + 64], prob.astype(BF16)))
                lse_ref[p, item, pl.ds(head, 1), :] = top + jnp.log(total)
            ctx_ref[p, rows] = jnp.concatenate(parts, axis=0).T.astype(BF16)
        return 0

    lax.fori_loop(0, 3, pair, 0)
    context = jnp.concatenate([ctx_ref[p] for p in range(3)], axis=1)
    for j in range(3):
        cols = slice(256 * j, 256 * j + 256)
        out = jnp.concatenate([heads_ref[p, 3, cols, :] for p in range(3)], axis=1)
        part_ref[:, cols] = dot_nt(context, out).astype(BF16)


def call_forward(counts, x, x_other, g1, b1, y, lows, high, qb, vb):
    rows = 2 * L
    return pl.pallas_call(
        forward_attention,
        in_specs=[SMEM] + [VMEM] * 4 + [SMEM] + [VMEM] * 7,
        out_specs=[VMEM] * 6,
        out_shape=[S((D, rows), BF16), S((3, 3, rows, 128), BF16), S((3, rows, 128), BF16),
                   S((3, 2, 2, L), F32), S((rows, D), BF16), S((3, 4, D, 128), BF16)],
        scratch_shapes=[pltpu.VMEM((rows, D), BF16), pltpu.VMEM((4, 3, D // 2, 128), BF16)],
        compiler_params=pltpu.CompilerParams(vmem_limit_bytes=50 << 20),
        cost_estimate=FREE,
        name="attention_forward",
    )(counts, x, x_other, g1, b1, y, *lows, high, qb, vb)


def middle(x_refs, own_ref, other_ref, ob_ref, half):
    mine, theirs = pl.ds(L * half, L), pl.ds(L - L * half, L)
    return x_refs[half][...].astype(F32) + (own_ref[mine, :].astype(F32) + other_ref[theirs, :].astype(F32)) + ob_ref[...]


def feed_forward(x_ref, x_other_ref, own_ref, other_ref, ob_ref, g2_ref, b2_ref, cot_ref, cot_other_ref, low_ref, high_ref, b1_ref,
                 mlp_ref, mlp_send_ref, gn2_ref, db_ref, dw_ref, n2_ref, n2t_ref, cots_ref, cott_ref, acc_ref, gacc_ref):
    step = pl.program_id(0)
    last = pl.num_programs(0) - 1

    @pl.when(step == 0)
    def _():
        for half in range(2):
            scaled, _ = normalize(middle((x_ref, x_other_ref), own_ref, other_ref, ob_ref, half))
            n2_ref[L * half : L * half + L] = (scaled * g2_ref[...] + b2_ref[...]).astype(BF16)
            cots_ref[L * half : L * half + L] = (cot_ref, cot_other_ref)[half][...]
        n2t_ref[...] = n2_ref[...].T
        cott_ref[...] = cots_ref[...].T
        acc_ref[...] = jnp.zeros_like(acc_ref)
        gacc_ref[...] = jnp.zeros_like(gacc_ref)

    first, second = (
        jnp.concatenate(
            [jnp.concatenate([low_ref[y, layer, 0], joined_rows(high_ref, (y, layer, 0), (), 4)], axis=0) for y in range(4)], axis=1
        )
        for layer in range(2)
    )
    hidden = dot_nn(n2_ref[...], first) + b1_ref[0]
    cdf = 0.5 * (1.0 + lax.erf(hidden * 0.7071067811865476))
    slope = cdf + hidden * (jnp.exp(-0.5 * hidden * hidden) * 0.3989422804014327)
    active = (hidden * cdf).astype(BF16)
    acc_ref[...] += dot_nt(active, second)
    grad_hidden = dot_nn(cots_ref[...], second) * slope
    db_ref[0] = row_sum(grad_hidden)
    grad_hidden = grad_hidden.astype(BF16)
    gacc_ref[...] += dot_nt(grad_hidden, first)
    for layer, grad in enumerate((dot_nn(n2t_ref[...], grad_hidden), dot_nn(cott_ref[...], active))):
        for x in range(4):
            for z in range(8):
                block = grad[96 * z + 24 * x : 96 * z + 24 * x + 24].astype(BF16)
                for y in range(4):
                    dw_ref[x, y, z, layer, 0] = block[:, 128 * y : 128 * y + 128]

    @pl.when(step == last)
    def _():
        mlp_ref[...] = acc_ref[:L].astype(BF16)
        mlp_send_ref[...] = acc_ref[L:].astype(BF16)
        gn2_ref[...] = gacc_ref[...].astype(BF16)


def call_feed_forward(x, x_other, own, other, ob, g2, b2, cot, cot_other, low, high, b1):
    rows = 2 * L
    half = pl.BlockSpec((L, D), lambda i: (0, 0))
    whole = pl.BlockSpec((rows, D), lambda i: (0, 0))
    line = pl.BlockSpec((1, D), lambda i: (0, 0))
    lows = pl.BlockSpec((4, 2, 1, D // 2, 128), lambda i: (0, 0, i, 0, 0))
    highs = pl.BlockSpec((4, 4, 2, 1, 4, 24, 128), lambda i: (0, 0, 0, i, 0, 0, 0))
    grads = pl.BlockSpec((4, 4, 8, 2, 1, 24, 128), lambda i: (0, 0, 0, 0, i, 0, 0))
    bias = pl.BlockSpec((1, 1, 512), lambda i: (i, 0, 0))
    return pl.pallas_call(
        feed_forward,
        grid=(3,),
        in_specs=[half, half, whole, whole, line, line, line, half, half, lows, highs, bias],
        out_specs=[half, half, whole, bias, grads],
        out_shape=[S((L, D), BF16), S((L, D), BF16), S((rows, D), BF16), S((3, 1, 512), F32), S((4, 4, 8, 2, 3, 24, 128), BF16)],
        scratch_shapes=[pltpu.VMEM((rows, D), BF16), pltpu.VMEM((D, rows), BF16), pltpu.VMEM((rows, D), BF16),
                        pltpu.VMEM((D, rows), BF16), pltpu.VMEM((rows, D), F32), pltpu.VMEM((rows, D), F32)],
        compiler_params=pltpu.CompilerParams(vmem_limit_bytes=58 << 20),
        cost_estimate=FREE,
        name="feed_forward",
    )(x, x_other, own, other, ob, g2, b2, cot, cot_other, low, high, b1)


def norm_two_back(x_refs, own_ref, other_ref, ob_ref, g2_ref, cot_refs, gown_ref, gother_ref, gb_ref, gbt_ref, gm_ref, sums_ref):
    for half in range(2):
        mine, theirs = pl.ds(L * half, L), pl.ds(L - L * half, L)
        scaled, inv = normalize(middle(x_refs, own_ref, other_ref, ob_ref, half))
        grad = gown_ref[mine, :].astype(F32) + gother_ref[theirs, :].astype(F32)
        cot = cot_refs[half][...].astype(F32)
        grad_mid = cot + norm_back(grad, g2_ref[...], scaled, inv)
        branch = grad_mid.astype(BF16)
        gb_ref[mine, :] = branch
        gbt_ref[:, L * half : L * half + L] = branch.T
        if half == 0:
            gm_ref[...] = grad_mid
            sums_ref[0:1, :] = row_sum(branch.astype(F32))
            sums_ref[1:2, :] = row_sum(grad * scaled)
            sums_ref[2:3, :] = row_sum(grad)
            sums_ref[3:4, :] = row_sum(cot)


def backward_pair(p, count_ref, heads_ref, qkv_ref, ctx_ref, lse_ref, gb_ref, gbt_ref, n1t_ref, joined_ref, qvb_ref):
    grad_context = dot_nn(gb_ref[...], heads_ref[p, 3]).astype(BF16)
    grad_out = dot_nn(gbt_ref[...], ctx_ref[p])
    for item in range(2):
        rows = slice(L * item, L * item + L)
        query, key, value = qkv_ref[0, p, rows], qkv_ref[1, p, rows], qkv_ref[2, p, rows]
        grad_ctx = grad_context[rows]
        key_t = key.T
        valid = lax.broadcasted_iota(jnp.int32, (L, L), 0) < count_ref[2 * item + count_ref[4]]
        grad_q, grad_k, grad_v = [], [], []
        for head in range(2):
            scores = jnp.where(valid, dot_nt(head_lanes(key, head), query), MASKED)
            prob = jnp.exp(scores - lse_ref[p, item, pl.ds(head, 1), :])
            grad_prob = dot_nt(head_lanes(value, head), grad_ctx)
            delta = row_sum(prob * grad_prob)
            grad_scores = (prob * (grad_prob - delta)).astype(BF16)
            grad_k.append(dot_nn(grad_scores, query))
            grad_v.append(dot_nn(prob.astype(BF16), grad_ctx))
            grad_q.append(dot_nn(key_t[64 * head : 64 * head + 64], grad_scores))
        joined_ref[p, rows, 0:128] = (jnp.concatenate(grad_q, axis=0).T * 0.125).astype(BF16)
        joined_ref[p, rows, 128:256] = pick_lanes(*grad_k).astype(BF16)
        joined_ref[p, rows, 256:384] = pick_lanes(*grad_v).astype(BF16)
    joined = joined_ref[p]
    sums = row_sum(joined.astype(F32))
    qvb_ref[p, 0:1, :] = sums[:, :128]
    qvb_ref[p, 1:2, :] = sums[:, 256:]
    grads = dot_nn(n1t_ref[...], joined)
    return grads[:, :128], grads[:, 128:256], grads[:, 256:], grad_out


def backward_attention(count_ref, x_ref, x_other_ref, own_ref, other_ref, ob_ref, g2_ref, cot_ref, cot_other_ref, gown_ref, gother_ref,
                       heads_ref, qkv_ref, ctx_ref, lse_ref, n1t_ref,
                       gm_ref, sums_ref, joined_ref, qvb_ref, dw_ref, gb_ref, gbt_ref, last_ref):
    norm_two_back((x_ref, x_other_ref), own_ref, other_ref, ob_ref, g2_ref, (cot_ref, cot_other_ref), gown_ref, gother_ref,
                  gb_ref, gbt_ref, gm_ref, sums_ref)

    def pair(p, _):
        grads = backward_pair(p, count_ref, heads_ref, qkv_ref, ctx_ref, lse_ref, gb_ref, gbt_ref, n1t_ref, joined_ref, qvb_ref)

        @pl.when(p < 2)
        def _():
            for i, grad in enumerate(grads):
                spread(dw_ref, 2 * (i // 2) + p, i % 2, grad)

        @pl.when(p == 2)
        def _():
            for i, grad in enumerate(grads):
                last_ref[i] = grad

        return 0

    lax.fori_loop(0, 3, pair, 0)
    for high in range(2):
        for low, grad in enumerate(twist(last_ref[2 * high], last_ref[2 * high + 1])):
            spread(dw_ref, 2 * high + low, 2, grad)


def spread(dw_ref, y, c, grad):
    for z in range(8):
        for x in range(4):
            at = 24 * (4 * z + x)
            dw_ref[y, x, z, c] = grad[at : at + 24].astype(BF16)


def call_backward(counts, x, x_other, own, other, ob, g2, cot, cot_other, gown, gother, heads, qkv, ctx, lse, n1t):
    rows = 2 * L
    return pl.pallas_call(
        backward_attention,
        in_specs=[SMEM] + [VMEM] * 15,
        out_specs=[VMEM] * 5,
        out_shape=[S((L, D), F32), S((4, D), F32), S((3, rows, 384), BF16), S((3, 2, 128), F32), S((4, 4, 8, 3, 24, 128), BF16)],
        scratch_shapes=[pltpu.VMEM((rows, D), BF16), pltpu.VMEM((D, rows), BF16), pltpu.VMEM((4, D, 128), F32)],
        compiler_params=pltpu.CompilerParams(vmem_limit_bytes=58 << 20),
        cost_estimate=FREE,
        name="attention_backward",
    )(counts, x, x_other, own, other, ob, g2, cot, cot_other, gown, gother, heads, qkv, ctx, lse, n1t)


def norm_one_grad(x_ref, x_other_ref, heads_ref, joined_ref, own_ref, send_ref, sums_ref):
    for half in range(2):
        rows = slice(L * half, L * half + L)
        grad = dot_nt(joined_ref[0, rows, :], wide(heads_ref, (0,), range(3)))
        for p in range(1, 3):
            grad = grad + dot_nt(joined_ref[p, rows, :], wide(heads_ref, (p,), range(3)))
        scaled, _ = normalize((x_ref, x_other_ref)[half][...].astype(F32))
        if half == 0:
            own_ref[...] = grad
            gain, shift = row_sum(grad * scaled), row_sum(grad)
        else:
            send_ref[...] = grad.astype(BF16)
            sums_ref[0:1, :] = gain + row_sum(grad * scaled)
            sums_ref[1:2, :] = shift + row_sum(grad)


def call_norm_one_grad(x, x_other, heads, joined):
    return pl.pallas_call(
        norm_one_grad,
        in_specs=[VMEM] * 4,
        out_specs=[VMEM] * 3,
        out_shape=[S((L, D), F32), S((L, D), BF16), S((2, D), F32)],
        compiler_params=pltpu.CompilerParams(vmem_limit_bytes=50 << 20),
        cost_estimate=FREE,
        name="norm_one_grad",
    )(x, x_other, heads, joined)


def norm_one_back(x_ref, g1_ref, gm_ref, own_ref, other_ref, fg_ref, low_ref):
    scaled, inv = normalize(x_ref[...].astype(F32))
    grad = own_ref[...] + other_ref[...].astype(F32)
    result = gm_ref[...] + norm_back(grad, g1_ref[...], scaled, inv)
    fg_ref[...] = result
    low_ref[...] = result.astype(BF16)


def call_norm_one_back(x, g1, gm, own, other):
    return pl.pallas_call(
        norm_one_back,
        grid=(1,),
        in_specs=[pl.BlockSpec((L, D), lambda i: (0, 0)), pl.BlockSpec((1, D), lambda i: (0, 0))]
        + [pl.BlockSpec((L, D), lambda i: (0, 0))] * 3,
        out_specs=[pl.BlockSpec((L, D), lambda i: (0, 0))] * 2,
        out_shape=[S((L, D), F32), S((L, D), BF16)],
        compiler_params=pltpu.CompilerParams(vmem_limit_bytes=40 << 20),
        cost_estimate=FREE,
        name="norm_one_back",
    )(x, g1, gm, own, other)


NAMES = ("z", "x", "yh", "core", "yl")
SIZES = (8, 4, 2, 2, 2)
DP = ("z", "x", "yh", "core")
Y = ("yh", "yl")
QUARTER = ("yh", "core")
ROWS = ("z", "yh", "core")


def after(values, *earlier):
    return pl.pallas_call(
        lambda *refs: None,
        in_specs=[pl.BlockSpec(memory_space=pl.ANY)] * (1 + len(earlier)),
        out_specs=pl.BlockSpec(memory_space=pl.ANY),
        out_shape=S(values.shape, values.dtype),
        input_output_aliases={0: 0},
        cost_estimate=FREE,
        name="after",
    )(values, *earlier)


def swap(values, axis, n, k):
    return lax.ppermute(values, axis, [(i, i ^ k) for i in range(n)])


def pick(values, index, axis=0):
    return lax.dynamic_index_in_dim(values, index, axis, keepdims=False)


def in_order(parts, index, axis):
    bit = 1
    while bit < len(parts):
        flip = (index & bit) != 0
        parts = [jnp.where(flip, parts[k ^ bit], parts[k]) for k in range(len(parts))]
        bit *= 2
    return jnp.stack(parts, axis=axis)


def gather(values, axis, n, index, place):
    return in_order([values] + [swap(values, axis, n, k) for k in range(1, n)], index, place)


def add_up(parts):
    total = parts[0].astype(F32)
    for part in parts[1:]:
        total = total + part.astype(F32)
    return total.astype(BF16)


def sent(parts, axis, n):
    return [parts[0]] + [swap(parts[k], axis, n, k) for k in range(1, n)]


def gather_rows(packed):
    c = packed.shape[1]
    return exchange(repeated(packed, 8).reshape(32, c, 6, 128), ROWS).reshape(8, 4, c, 6, 128)


def whole_rows(got):
    return got.transpose(2, 0, 1, 3, 4).reshape(got.shape[2], 8, 24, 128)


def copies(values, axis, n):
    return [values] + [swap(values, axis, n, k) for k in range(1, n)]


def assemble(at_ref, *refs):
    lows, highs, (low_ref, rest_low_ref, high_ref, rest_high_ref) = refs[:4], refs[4:8], refs[8:]
    for k in range(4):
        x, y = at_ref[0] ^ k, at_ref[1] ^ k
        low_ref[:, :, x] = lows[k][:3]
        rest_low_ref[:, :, x] = lows[k][3:]
        for copy in range(4):
            high_ref[copy, y] = highs[k][:3]
            rest_high_ref[copy, y] = highs[k][3:]


def gather_half(rows, at):
    parts = copies(rows[:, :4], "x", 4) + copies(rows[:, 4:], Y, 4)
    low, rest_low, high, rest_high = pl.pallas_call(
        assemble,
        in_specs=[SMEM] + [VMEM] * 8,
        out_specs=[VMEM] * 4,
        out_shape=[S((3, 4, 4, 24, 128), BF16), S((6, 4, 4, 24, 128), BF16),
                   S((4, 4, 3, 4, 24, 128), BF16), S((4, 4, 6, 4, 24, 128), BF16)],
        compiler_params=pltpu.CompilerParams(vmem_limit_bytes=40 << 20),
        cost_estimate=FREE,
        name="assemble",
    )(jnp.stack([at["x"], at["y"]]), *parts)
    return low.reshape(3, 384, 128), rest_low.reshape(6, 384, 128), high, rest_high


def repeated(values, n):
    return jnp.broadcast_to(values[None], (n, *values.shape))


def exchange(values, axis):
    return lax.all_to_all(values, axis, split_axis=0, concat_axis=0, tiled=True)


def scatter_rows(rows, extra):
    c = rows.shape[1]
    cut = rows.reshape(8, c, 4, 6, 128).transpose(0, 2, 1, 3, 4).reshape(32, c, 6, 128)
    quarter = pick(extra.astype(BF16).reshape(4, c, 2, 128), lax.axis_index("yh") * 2 + lax.axis_index("core"))
    cut = jnp.concatenate([cut, repeated(quarter, 32)], axis=2)
    got = jnp.sum(exchange(cut, ROWS).reshape(8, 4, c, 8, 128).astype(F32), axis=0)
    return cut, got[:, :, :6], got[:, :, 6:].reshape(72, 128)


def sum_over(values, axis, n):
    return pair_sum(copies(values, axis, n))


def pair_sum(parts):
    while len(parts) > 1:
        parts = [first + second for first, second in zip(parts[::2], parts[1::2])]
    return parts[0]


def sum_and_join(got_ref, small_ref, out_ref):
    small = small_ref[...].astype(BF16)
    for x in range(4):
        total = got_ref[0, x].astype(F32)
        for part in range(1, 4):
            total = total + got_ref[part, x].astype(F32)
        out_ref[x, :576] = total.reshape(576, 128).astype(BF16)
        out_ref[x, 576:] = small


def call_sum_and_join(got, small):
    return pl.pallas_call(
        sum_and_join,
        in_specs=[VMEM] * 2,
        out_specs=VMEM,
        out_shape=S((4, 648, 128), BF16),
        compiler_params=pltpu.CompilerParams(vmem_limit_bytes=40 << 20),
        cost_estimate=FREE,
        name="sum_and_join",
    )(got, small)


def place_items(at_ref, out_ref, out_other_ref, fg_ref, fg_other_ref, cut_ref, layer_ref, features_ref):
    del at_ref, cut_ref

    @pl.when(pl.program_id(0) == 0)
    def _():
        layer_ref[0] = out_ref[...]
        features_ref[0] = fg_ref[...]

    @pl.when(pl.program_id(0) == 1)
    def _():
        layer_ref[0] = out_other_ref[...]
        features_ref[0] = fg_other_ref[...].astype(F32)


def call_place_items(at, out, out_other, fg, fg_other, cut):
    whole = pl.BlockSpec((L, D), lambda i, at: (0, 0))
    one = pl.BlockSpec((1, L, D), lambda i, at: (at[0] ^ i, 0, 0))
    return pl.pallas_call(
        place_items,
        grid_spec=pltpu.PrefetchScalarGridSpec(
            num_scalar_prefetch=1,
            grid=(2,),
            in_specs=[whole] * 4 + [pl.BlockSpec(memory_space=pl.ANY)],
            out_specs=[one, one],
        ),
        out_shape=[S((2, L, D), BF16), S((2, L, D), F32)],
        compiler_params=pltpu.CompilerParams(vmem_limit_bytes=40 << 20),
        cost_estimate=LONG,
        name="place_items",
    )(at, out, out_other, fg, fg_other, cut)


def on_core(values, at, axis):
    zero = jnp.zeros_like(values)
    return jnp.stack([jnp.where(at["core"] == 0, values, zero), jnp.where(at["core"] == 0, zero, values)], axis=axis)


def pack(query_key_value_weight, out_weight, fc1_weight, fc2_weight):
    kinds = jnp.concatenate(
        [query_key_value_weight.reshape(6, 3, 2, 3, 64), out_weight.T.reshape(6, 1, 2, 3, 64)], axis=1
    ).reshape(6, 2, 2, 2, 3, 64)
    two = kinds[:, :, :, :, :2].reshape(6, 2, 2, 2, 128).transpose(1, 3, 2, 0, 4)
    third = kinds[:, :, :, :, 2].transpose(1, 3, 0, 2, 4).reshape(2, 2, 1, 6, 128)
    first = fc1_weight.reshape(6, 2, 2, 3, 128).transpose(1, 2, 3, 0, 4)
    second = fc2_weight.T.reshape(6, 2, 2, 3, 128).transpose(1, 2, 3, 0, 4)
    return jnp.concatenate([two, third, first, second], axis=2).reshape(4, 9, 6, 128)


def unpack(attention, fc):
    attention = attention.reshape(2, 2, 3, 6, 128)
    two = attention[:, :, :2].reshape(2, 2, 2, 6, 2, 64)
    third = attention[:, :, 2].reshape(2, 2, 6, 2, 64).transpose(0, 1, 3, 2, 4).reshape(2, 2, 2, 6, 1, 64)
    kinds = jnp.concatenate([two, third], axis=4).transpose(0, 2, 3, 1, 4, 5).reshape(4, 6, 384)
    first = fc[:, :3].transpose(2, 0, 1, 3).reshape(6, 1536)
    second = fc[:, 3:].transpose(0, 1, 3, 2).reshape(1536, 6)
    return kinds[:3].transpose(1, 0, 2), kinds[3].T, first, second


def on_device(
    features, patch_counts, ln1_gain, ln1_bias, query_key_value_weight, qv_bias, out_weight, out_bias,
    ln2_gain, ln2_bias, fc1_weight, fc1_bias, fc2_weight, fc2_bias, cotangent,
):
    at = {name: lax.axis_index(name) for name in NAMES}
    at["y"] = at["yh"] * 2 + at["yl"]
    row = lambda v: v.reshape(1, -1)

    rows = gather_rows(pack(query_key_value_weight, out_weight, fc1_weight, fc2_weight))

    item, cot = pick(features, at["yl"]), pick(cotangent, at["yl"])
    item_other, cot_other = swap(item, "core", 2, 1), swap(cot, "core", 2, 1)
    counts = jnp.concatenate([patch_counts, swap(patch_counts, "core", 2, 1), at["yl"].reshape(1)])
    biases = gather(jnp.concatenate([qv_bias.reshape(-1), fc1_bias]).reshape(18, 128), "yl", 2, at["yl"], 0)
    heads_bias = pick(biases[:, :6].reshape(2, 2, 2, 3, 64), at["core"], 2)
    heads_bias = jnp.stack(
        [heads_bias[0, :, :2].reshape(2, 128), heads_bias[1, :, :2].reshape(2, 128), heads_bias[:, :, 2].transpose(1, 0, 2).reshape(2, 128)]
    )
    hidden_bias = pick(biases[:, 6:].reshape(2, 2, 2, 3, 128), at["core"], 2).transpose(2, 1, 0, 3).reshape(3, 1, 512)
    query_bias, value_bias = heads_bias[:, 0], heads_bias[:, 1]
    ob, g1, g2 = row(out_bias), row(ln1_gain), row(ln2_gain)
    rows = whole_rows(after(rows, item_other, cot_other, counts, query_bias, value_bias, hidden_bias))
    low, rest_low, high, rest_high = gather_half(rows, at)
    lows, attention_high = copies(low, Y, 4), exchange(high, "x")
    fc_low, fc_high = lax.all_gather(rest_low, Y), exchange(rest_high, "x")
    n1t, qkv, context, log_total, own, heads = call_forward(
        counts, item, item_other, g1, row(ln1_bias), at["y"].reshape(1), lows, attention_high, query_bias, value_bias
    )
    other = swap(own, "core", 2, 1)
    mlp, mlp_send, gown, hidden_sums, fc_local = call_feed_forward(
        item, item_other, own, other, ob, g2, row(ln2_bias), cot, cot_other,
        fc_low.reshape(4, 2, 3, D // 2, 128), fc_high.reshape(4, 4, 2, 3, 4, 24, 128), hidden_bias
    )
    mid = item.astype(F32) + (own[:L].astype(F32) + other[L:].astype(F32)) + out_bias
    out_rows = (mid + (mlp.astype(F32) + swap(mlp_send, "core", 2, 1).astype(F32)) + fc2_bias).astype(BF16)
    out_other = swap(out_rows, "yl", 2, 1)
    gother = after(swap(gown, "core", 2, 1), out_rows)
    fc = lax.psum_scatter(fc_local.reshape(4, 4, 8, 6, 24, 128), "x")
    grad_mid, sums_two, joined, qv, grads = call_backward(
        counts, item, item_other, own, other, ob, g2, cot, cot_other, gown, gother, heads, qkv, context, log_total, n1t
    )
    got = exchange(after(grads, out_other), Y)
    grad_one, grad_send, sums_one = call_norm_one_grad(item, item_other, heads, joined)

    qv = jnp.concatenate([qv[:2].reshape(2, 2, 2, 64), qv[2].reshape(2, 2, 64).transpose(1, 0, 2)[:, :, None]], axis=2)
    qv = on_core(qv.transpose(1, 0, 2, 3), at, 2).reshape(12, 128)
    hidden_sums = on_core(hidden_sums.reshape(3, 2, 2, 128).transpose(2, 1, 0, 3), at, 2).reshape(24, 128)
    small = jnp.concatenate([sums_one.reshape(12, 128), sums_two.reshape(24, 128), qv, hidden_sums])

    pieces = after(fc, sums_one)
    pieces = [pick(pieces, at["y"] ^ k) for k in range(4)]
    small = small + swap(small, "core", 2, 1)
    parts = copies(small, Y, 4)
    grad_other = after(swap(grad_send, "core", 2, 1), pieces[3])
    fg, fg_low = call_norm_one_back(item, g1, grad_mid, grad_one, grad_other)
    fg_other = swap(fg_low, "yl", 2, 1)
    got = after(got, fg_low)
    parts[1] = after(parts[1], got)
    small = pair_sum(parts)
    got = exchange(call_sum_and_join(got, small), "x")
    pieces = sent(pieces, Y, 4)
    fc_rows = add_up(pieces)
    got = jnp.sum(after(got, fc_rows).astype(F32), axis=0)
    attention_rows = got[:576].astype(BF16).reshape(8, 3, 24, 128)
    cut, owned, small = scatter_rows(jnp.concatenate([attention_rows, fc_rows], axis=1), got[576:])
    layer_out, features_grad = call_place_items(at["yl"].reshape(1), out_rows, out_other, fg, fg_other, cut)
    qkv_grad, out_grad, fc1_grad, fc2_grad = unpack(owned[:, :3], owned[:, 3:])

    sums = small[:36].reshape(6, D)
    qv_grad = pick(small[36:48].reshape(2, 2, 384), at["yl"], 1)
    hidden_grad = pick(small[48:].reshape(2, 1536), at["yl"])
    return (
        layer_out, features_grad, sums[0], sums[1], qkv_grad, qv_grad, out_grad, sums[2], sums[3], sums[4],
        fc1_grad, hidden_grad, fc2_grad, sums[5],
    )


def solution(mesh):
    five = Mesh(mesh.devices.reshape(SIZES), NAMES)
    return jax.shard_map(
        on_device,
        mesh=five,
        in_specs=(
            P(DP, None, None), P(DP), P(), P(), P(DP, None, "yl"), P(None, "yl"), P("yl", DP), P(),
            P(), P(), P(DP, "yl"), P("yl"), P("yl", DP), P(), P(DP, None, None),
        ),
        out_specs=(
            P(DP, None, None), P(DP, None, None), P(), P(), P(DP, None, "yl"), P(None, "yl"), P("yl", DP), P(),
            P(), P(), P(DP, "yl"), P("yl"), P("yl", DP), P(),
        ),
        check_vma=False,
    )
```

```python
import jax
import jax.numpy as jnp
from jax import lax
from jax.experimental import pallas as pl
from jax.experimental.pallas import tpu as pltpu
from jax.sharding import Mesh, PartitionSpec as P

F32 = jnp.float32
BF16 = jnp.bfloat16
EPS = 1e-06
MASKED = -1e30
VMEM = pl.BlockSpec(memory_space=pltpu.VMEM)
SMEM = pl.BlockSpec(memory_space=pltpu.SMEM)
S = jax.ShapeDtypeStruct
L = 512
D = 768
FREE = pl.CostEstimate(flops=1000, bytes_accessed=1000, transcendentals=0)
LONG = pl.CostEstimate(flops=10**11, bytes_accessed=10**8, transcendentals=0)


def dot_nn(a, b):
    return lax.dot_general(a, b, (((1,), (0,)), ((), ())), preferred_element_type=F32)


def dot_nt(a, b):
    return lax.dot_general(a, b, (((1,), (1,)), ((), ())), preferred_element_type=F32)


def normalize(values):
    row_mean = jnp.mean(values, axis=-1, keepdims=True)
    centred = values - row_mean
    inv_std = lax.rsqrt(jnp.mean(centred * centred, axis=-1, keepdims=True) + EPS)
    return centred * inv_std, inv_std


def norm_back(grad_normed, gain_row, scaled, inv_std):
    grad_scaled = grad_normed * gain_row
    first_mean = jnp.mean(grad_scaled, axis=-1, keepdims=True)
    second_mean = jnp.mean(grad_scaled * scaled, axis=-1, keepdims=True)
    return inv_std * (grad_scaled - first_mean - scaled * second_mean)


def row_sum(values):
    return jnp.sum(values, axis=0, keepdims=True)


def head_lanes(values, head):
    lane = lax.broadcasted_iota(jnp.int32, values.shape, 1)
    return jnp.where((lane >= 64) == (head == 1), values, jnp.zeros_like(values))


def pick_lanes(first, second):
    lane = lax.broadcasted_iota(jnp.int32, first.shape, 1)
    return jnp.where(lane < 64, first, second)


def joined_rows(ref, lead, tail, count):
    return jnp.concatenate([ref[(x, *lead, z, *tail)].astype(F32) for z in range(count) for x in range(4)], axis=0).astype(BF16)


def twist(first, second):
    return (
        jnp.concatenate([first[:, :64], second[:, :64]], axis=1),
        jnp.concatenate([first[:, 64:], second[:, 64:]], axis=1),
    )


def wide(ref, lead, kinds):
    return jnp.concatenate([ref[(*lead, k)] for k in kinds], axis=1)


def forward_attention(count_ref, x_ref, x_other_ref, g1_ref, b1_ref, y_ref, low0_ref, low1_ref, low2_ref, low3_ref, high_ref, qb_ref, vb_ref,
                      n1t_ref, qkv_ref, ctx_ref, lse_ref, part_ref, heads_ref, n1_ref, low_ref):
    for half, ref in enumerate((x_ref, x_other_ref)):
        scaled, _ = normalize(ref[...].astype(F32))
        normed = (scaled * g1_ref[...] + b1_ref[...]).astype(BF16)
        n1_ref[L * half : L * half + L] = normed
        n1t_ref[:, L * half : L * half + L] = normed.T
    for k, ref in enumerate((low0_ref, low1_ref, low2_ref, low3_ref)):
        low_ref[y_ref[0] ^ k] = ref[...]

    def weight(half, p, c):
        return jnp.concatenate([low_ref[2 * half + p, c], joined_rows(high_ref, (2 * half + p, c), (), 4)], axis=0)

    for half in range(2):
        for p in range(2):
            for kind in range(2):
                heads_ref[p, 2 * half + kind] = weight(half, p, kind)
        heads_ref[2, 2 * half], heads_ref[2, 2 * half + 1] = twist(weight(half, 0, 2), weight(half, 1, 2))

    def pair(p, _):
        projected = dot_nn(n1_ref[...], wide(heads_ref, (p,), range(3)))
        queries = (projected[:, :128] + qb_ref[pl.ds(p, 1), :]).astype(BF16) * BF16(0.125)
        keys = projected[:, 128:256].astype(BF16)
        values = (projected[:, 256:] + vb_ref[pl.ds(p, 1), :]).astype(BF16)
        qkv_ref[0, p] = queries
        qkv_ref[1, p] = keys
        qkv_ref[2, p] = values
        for item in range(2):
            rows = slice(L * item, L * item + L)
            query, key, value_t = queries[rows], keys[rows], values[rows].T
            valid = lax.broadcasted_iota(jnp.int32, (L, L), 0) < count_ref[2 * item + count_ref[4]]
            parts = []
            for head in range(2):
                scores = jnp.where(valid, dot_nt(head_lanes(key, head), query), MASKED)
                top = jnp.max(scores, axis=0, keepdims=True)
                shifted = jnp.exp(scores - top)
                total = row_sum(shifted)
                prob = shifted * (1.0 / total)
                parts.append(dot_nn(value_t[64 * head : 64 * head + 64], prob.astype(BF16)))
                lse_ref[p, item, pl.ds(head, 1), :] = top + jnp.log(total)
            ctx_ref[p, rows] = jnp.concatenate(parts, axis=0).T.astype(BF16)
        return 0

    lax.fori_loop(0, 3, pair, 0)
    context = jnp.concatenate([ctx_ref[p] for p in range(3)], axis=1)
    for j in range(3):
        cols = slice(256 * j, 256 * j + 256)
        out = jnp.concatenate([heads_ref[p, 3, cols, :] for p in range(3)], axis=1)
        part_ref[:, cols] = dot_nt(context, out).astype(BF16)


def call_forward(counts, x, x_other, g1, b1, y, lows, high, qb, vb):
    rows = 2 * L
    return pl.pallas_call(
        forward_attention,
        in_specs=[SMEM] + [VMEM] * 4 + [SMEM] + [VMEM] * 7,
        out_specs=[VMEM] * 6,
        out_shape=[S((D, rows), BF16), S((3, 3, rows, 128), BF16), S((3, rows, 128), BF16),
                   S((3, 2, 2, L), F32), S((rows, D), BF16), S((3, 4, D, 128), BF16)],
        scratch_shapes=[pltpu.VMEM((rows, D), BF16), pltpu.VMEM((4, 3, D // 2, 128), BF16)],
        compiler_params=pltpu.CompilerParams(vmem_limit_bytes=50 << 20),
        cost_estimate=FREE,
        name="attention_forward",
    )(counts, x, x_other, g1, b1, y, *lows, high, qb, vb)


def middle(x_refs, own_ref, other_ref, ob_ref, half):
    mine, theirs = pl.ds(L * half, L), pl.ds(L - L * half, L)
    return x_refs[half][...].astype(F32) + (own_ref[mine, :].astype(F32) + other_ref[theirs, :].astype(F32)) + ob_ref[...]


def feed_forward(x_ref, x_other_ref, own_ref, other_ref, ob_ref, g2_ref, b2_ref, cot_ref, cot_other_ref, low_ref, high_ref, b1_ref,
                 mlp_ref, mlp_send_ref, gn2_ref, db_ref, dw_ref, n2_ref, n2t_ref, cots_ref, cott_ref, acc_ref, gacc_ref):
    step = pl.program_id(0)
    last = pl.num_programs(0) - 1

    @pl.when(step == 0)
    def _():
        for half in range(2):
            scaled, _ = normalize(middle((x_ref, x_other_ref), own_ref, other_ref, ob_ref, half))
            n2_ref[L * half : L * half + L] = (scaled * g2_ref[...] + b2_ref[...]).astype(BF16)
            cots_ref[L * half : L * half + L] = (cot_ref, cot_other_ref)[half][...]
        n2t_ref[...] = n2_ref[...].T
        cott_ref[...] = cots_ref[...].T
        acc_ref[...] = jnp.zeros_like(acc_ref)
        gacc_ref[...] = jnp.zeros_like(gacc_ref)

    first, second = (
        jnp.concatenate(
            [jnp.concatenate([low_ref[y, layer, 0], joined_rows(high_ref, (y, layer, 0), (), 4)], axis=0) for y in range(4)], axis=1
        )
        for layer in range(2)
    )
    hidden = dot_nn(n2_ref[...], first) + b1_ref[0]
    cdf = 0.5 * (1.0 + lax.erf(hidden * 0.7071067811865476))
    slope = cdf + hidden * (jnp.exp(-0.5 * hidden * hidden) * 0.3989422804014327)
    active = (hidden * cdf).astype(BF16)
    acc_ref[...] += dot_nt(active, second)
    grad_hidden = dot_nn(cots_ref[...], second) * slope
    db_ref[0] = row_sum(grad_hidden)
    grad_hidden = grad_hidden.astype(BF16)
    gacc_ref[...] += dot_nt(grad_hidden, first)
    for layer, grad in enumerate((dot_nn(n2t_ref[...], grad_hidden), dot_nn(cott_ref[...], active))):
        for x in range(4):
            for z in range(8):
                block = grad[96 * z + 24 * x : 96 * z + 24 * x + 24].astype(BF16)
                for y in range(4):
                    dw_ref[x, y, z, layer, 0] = block[:, 128 * y : 128 * y + 128]

    @pl.when(step == last)
    def _():
        mlp_ref[...] = acc_ref[:L].astype(BF16)
        mlp_send_ref[...] = acc_ref[L:].astype(BF16)
        gn2_ref[...] = gacc_ref[...].astype(BF16)


def call_feed_forward(x, x_other, own, other, ob, g2, b2, cot, cot_other, low, high, b1):
    rows = 2 * L
    half = pl.BlockSpec((L, D), lambda i: (0, 0))
    whole = pl.BlockSpec((rows, D), lambda i: (0, 0))
    line = pl.BlockSpec((1, D), lambda i: (0, 0))
    lows = pl.BlockSpec((4, 2, 1, D // 2, 128), lambda i: (0, 0, i, 0, 0))
    highs = pl.BlockSpec((4, 4, 2, 1, 4, 24, 128), lambda i: (0, 0, 0, i, 0, 0, 0))
    grads = pl.BlockSpec((4, 4, 8, 2, 1, 24, 128), lambda i: (0, 0, 0, 0, i, 0, 0))
    bias = pl.BlockSpec((1, 1, 512), lambda i: (i, 0, 0))
    return pl.pallas_call(
        feed_forward,
        grid=(3,),
        in_specs=[half, half, whole, whole, line, line, line, half, half, lows, highs, bias],
        out_specs=[half, half, whole, bias, grads],
        out_shape=[S((L, D), BF16), S((L, D), BF16), S((rows, D), BF16), S((3, 1, 512), F32), S((4, 4, 8, 2, 3, 24, 128), BF16)],
        scratch_shapes=[pltpu.VMEM((rows, D), BF16), pltpu.VMEM((D, rows), BF16), pltpu.VMEM((rows, D), BF16),
                        pltpu.VMEM((D, rows), BF16), pltpu.VMEM((rows, D), F32), pltpu.VMEM((rows, D), F32)],
        compiler_params=pltpu.CompilerParams(vmem_limit_bytes=58 << 20),
        cost_estimate=FREE,
        name="feed_forward",
    )(x, x_other, own, other, ob, g2, b2, cot, cot_other, low, high, b1)


def norm_two_back(x_refs, own_ref, other_ref, ob_ref, g2_ref, cot_refs, gown_ref, gother_ref, gb_ref, gbt_ref, gm_ref, sums_ref):
    for half in range(2):
        mine, theirs = pl.ds(L * half, L), pl.ds(L - L * half, L)
        scaled, inv = normalize(middle(x_refs, own_ref, other_ref, ob_ref, half))
        grad = gown_ref[mine, :].astype(F32) + gother_ref[theirs, :].astype(F32)
        cot = cot_refs[half][...].astype(F32)
        grad_mid = cot + norm_back(grad, g2_ref[...], scaled, inv)
        branch = grad_mid.astype(BF16)
        gb_ref[mine, :] = branch
        gbt_ref[:, L * half : L * half + L] = branch.T
        if half == 0:
            gm_ref[...] = grad_mid
            sums_ref[0:1, :] = row_sum(branch.astype(F32))
            sums_ref[1:2, :] = row_sum(grad * scaled)
            sums_ref[2:3, :] = row_sum(grad)
            sums_ref[3:4, :] = row_sum(cot)


def backward_pair(p, count_ref, heads_ref, qkv_ref, ctx_ref, lse_ref, gb_ref, gbt_ref, n1t_ref, joined_ref, qvb_ref):
    grad_context = dot_nn(gb_ref[...], heads_ref[p, 3]).astype(BF16)
    grad_out = dot_nn(gbt_ref[...], ctx_ref[p])
    for item in range(2):
        rows = slice(L * item, L * item + L)
        query, key, value = qkv_ref[0, p, rows], qkv_ref[1, p, rows], qkv_ref[2, p, rows]
        grad_ctx = grad_context[rows]
        key_t = key.T
        valid = lax.broadcasted_iota(jnp.int32, (L, L), 0) < count_ref[2 * item + count_ref[4]]
        grad_q, grad_k, grad_v = [], [], []
        for head in range(2):
            scores = jnp.where(valid, dot_nt(head_lanes(key, head), query), MASKED)
            prob = jnp.exp(scores - lse_ref[p, item, pl.ds(head, 1), :])
            grad_prob = dot_nt(head_lanes(value, head), grad_ctx)
            delta = row_sum(prob * grad_prob)
            grad_scores = (prob * (grad_prob - delta)).astype(BF16)
            grad_k.append(dot_nn(grad_scores, query))
            grad_v.append(dot_nn(prob.astype(BF16), grad_ctx))
            grad_q.append(dot_nn(key_t[64 * head : 64 * head + 64], grad_scores))
        joined_ref[p, rows, 0:128] = (jnp.concatenate(grad_q, axis=0).T * 0.125).astype(BF16)
        joined_ref[p, rows, 128:256] = pick_lanes(*grad_k).astype(BF16)
        joined_ref[p, rows, 256:384] = pick_lanes(*grad_v).astype(BF16)
    joined = joined_ref[p]
    sums = row_sum(joined.astype(F32))
    qvb_ref[p, 0:1, :] = sums[:, :128]
    qvb_ref[p, 1:2, :] = sums[:, 256:]
    grads = dot_nn(n1t_ref[...], joined)
    return grads[:, :128], grads[:, 128:256], grads[:, 256:], grad_out


def backward_attention(count_ref, x_ref, x_other_ref, own_ref, other_ref, ob_ref, g2_ref, cot_ref, cot_other_ref, gown_ref, gother_ref,
                       heads_ref, qkv_ref, ctx_ref, lse_ref, n1t_ref,
                       gm_ref, sums_ref, joined_ref, qvb_ref, dw_ref, gb_ref, gbt_ref, last_ref):
    norm_two_back((x_ref, x_other_ref), own_ref, other_ref, ob_ref, g2_ref, (cot_ref, cot_other_ref), gown_ref, gother_ref,
                  gb_ref, gbt_ref, gm_ref, sums_ref)

    def pair(p, _):
        grads = backward_pair(p, count_ref, heads_ref, qkv_ref, ctx_ref, lse_ref, gb_ref, gbt_ref, n1t_ref, joined_ref, qvb_ref)

        @pl.when(p < 2)
        def _():
            for i, grad in enumerate(grads):
                spread(dw_ref, 2 * (i // 2) + p, i % 2, grad)

        @pl.when(p == 2)
        def _():
            for i, grad in enumerate(grads):
                last_ref[i] = grad

        return 0

    lax.fori_loop(0, 3, pair, 0)
    for high in range(2):
        for low, grad in enumerate(twist(last_ref[2 * high], last_ref[2 * high + 1])):
            spread(dw_ref, 2 * high + low, 2, grad)


def spread(dw_ref, y, c, grad):
    for z in range(8):
        for x in range(4):
            at = 24 * (4 * z + x)
            dw_ref[y, x, z, c] = grad[at : at + 24].astype(BF16)


def call_backward(counts, x, x_other, own, other, ob, g2, cot, cot_other, gown, gother, heads, qkv, ctx, lse, n1t):
    rows = 2 * L
    return pl.pallas_call(
        backward_attention,
        in_specs=[SMEM] + [VMEM] * 15,
        out_specs=[VMEM] * 5,
        out_shape=[S((L, D), F32), S((4, D), F32), S((3, rows, 384), BF16), S((3, 2, 128), F32), S((4, 4, 8, 3, 24, 128), BF16)],
        scratch_shapes=[pltpu.VMEM((rows, D), BF16), pltpu.VMEM((D, rows), BF16), pltpu.VMEM((4, D, 128), F32)],
        compiler_params=pltpu.CompilerParams(vmem_limit_bytes=58 << 20),
        cost_estimate=FREE,
        name="attention_backward",
    )(counts, x, x_other, own, other, ob, g2, cot, cot_other, gown, gother, heads, qkv, ctx, lse, n1t)


def norm_one_grad(x_ref, x_other_ref, heads_ref, joined_ref, own_ref, send_ref, sums_ref):
    for half in range(2):
        rows = slice(L * half, L * half + L)
        grad = dot_nt(joined_ref[0, rows, :], wide(heads_ref, (0,), range(3)))
        for p in range(1, 3):
            grad = grad + dot_nt(joined_ref[p, rows, :], wide(heads_ref, (p,), range(3)))
        scaled, _ = normalize((x_ref, x_other_ref)[half][...].astype(F32))
        if half == 0:
            own_ref[...] = grad
            gain, shift = row_sum(grad * scaled), row_sum(grad)
        else:
            send_ref[...] = grad.astype(BF16)
            sums_ref[0:1, :] = gain + row_sum(grad * scaled)
            sums_ref[1:2, :] = shift + row_sum(grad)


def call_norm_one_grad(x, x_other, heads, joined):
    return pl.pallas_call(
        norm_one_grad,
        in_specs=[VMEM] * 4,
        out_specs=[VMEM] * 3,
        out_shape=[S((L, D), F32), S((L, D), BF16), S((2, D), F32)],
        compiler_params=pltpu.CompilerParams(vmem_limit_bytes=50 << 20),
        cost_estimate=FREE,
        name="norm_one_grad",
    )(x, x_other, heads, joined)


def norm_one_back(x_ref, g1_ref, gm_ref, own_ref, other_ref, fg_ref, low_ref):
    scaled, inv = normalize(x_ref[...].astype(F32))
    grad = own_ref[...] + other_ref[...].astype(F32)
    result = gm_ref[...] + norm_back(grad, g1_ref[...], scaled, inv)
    fg_ref[...] = result
    low_ref[...] = result.astype(BF16)


def call_norm_one_back(x, g1, gm, own, other):
    return pl.pallas_call(
        norm_one_back,
        grid=(1,),
        in_specs=[pl.BlockSpec((L, D), lambda i: (0, 0)), pl.BlockSpec((1, D), lambda i: (0, 0))]
        + [pl.BlockSpec((L, D), lambda i: (0, 0))] * 3,
        out_specs=[pl.BlockSpec((L, D), lambda i: (0, 0))] * 2,
        out_shape=[S((L, D), F32), S((L, D), BF16)],
        compiler_params=pltpu.CompilerParams(vmem_limit_bytes=40 << 20),
        cost_estimate=FREE,
        name="norm_one_back",
    )(x, g1, gm, own, other)


NAMES = ("z", "x", "yh", "core", "yl")
SIZES = (8, 4, 2, 2, 2)
DP = ("z", "x", "yh", "core")
Y = ("yh", "yl")
QUARTER = ("yh", "core")
ROWS = ("z", "yh", "core")


def after(values, *earlier):
    return pl.pallas_call(
        lambda *refs: None,
        in_specs=[pl.BlockSpec(memory_space=pl.ANY)] * (1 + len(earlier)),
        out_specs=pl.BlockSpec(memory_space=pl.ANY),
        out_shape=S(values.shape, values.dtype),
        input_output_aliases={0: 0},
        cost_estimate=FREE,
        name="after",
    )(values, *earlier)


def swap(values, axis, n, k):
    return lax.ppermute(values, axis, [(i, i ^ k) for i in range(n)])


def pick(values, index, axis=0):
    return lax.dynamic_index_in_dim(values, index, axis, keepdims=False)


def in_order(parts, index, axis):
    bit = 1
    while bit < len(parts):
        flip = (index & bit) != 0
        parts = [jnp.where(flip, parts[k ^ bit], parts[k]) for k in range(len(parts))]
        bit *= 2
    return jnp.stack(parts, axis=axis)


def gather(values, axis, n, index, place):
    return in_order([values] + [swap(values, axis, n, k) for k in range(1, n)], index, place)


def add_up(parts):
    total = parts[0].astype(F32)
    for part in parts[1:]:
        total = total + part.astype(F32)
    return total.astype(BF16)


def sent(parts, axis, n):
    return [parts[0]] + [swap(parts[k], axis, n, k) for k in range(1, n)]


def gather_rows(packed):
    c = packed.shape[1]
    return exchange(repeated(packed, 8).reshape(32, c, 6, 128), ROWS).reshape(8, 4, c, 6, 128)


def whole_rows(got):
    return got.transpose(2, 0, 1, 3, 4).reshape(got.shape[2], 8, 24, 128)


def copies(values, axis, n):
    return [values] + [swap(values, axis, n, k) for k in range(1, n)]


def assemble(at_ref, *refs):
    lows, highs, (low_ref, rest_low_ref, high_ref, rest_high_ref) = refs[:4], refs[4:8], refs[8:]
    for k in range(4):
        x, y = at_ref[0] ^ k, at_ref[1] ^ k
        low_ref[:, :, x] = lows[k][:3]
        rest_low_ref[:, :, x] = lows[k][3:]
        for copy in range(4):
            high_ref[copy, y] = highs[k][:3]
            rest_high_ref[copy, y] = highs[k][3:]


def gather_half(rows, at):
    parts = copies(rows[:, :4], "x", 4) + copies(rows[:, 4:], Y, 4)
    low, rest_low, high, rest_high = pl.pallas_call(
        assemble,
        in_specs=[SMEM] + [VMEM] * 8,
        out_specs=[VMEM] * 4,
        out_shape=[S((3, 4, 4, 24, 128), BF16), S((6, 4, 4, 24, 128), BF16),
                   S((4, 4, 3, 4, 24, 128), BF16), S((4, 4, 6, 4, 24, 128), BF16)],
        compiler_params=pltpu.CompilerParams(vmem_limit_bytes=40 << 20),
        cost_estimate=FREE,
        name="assemble",
    )(jnp.stack([at["x"], at["y"]]), *parts)
    return low.reshape(3, 384, 128), rest_low.reshape(6, 384, 128), high, rest_high


def repeated(values, n):
    return jnp.broadcast_to(values[None], (n, *values.shape))


def exchange(values, axis):
    return lax.all_to_all(values, axis, split_axis=0, concat_axis=0, tiled=True)


def sum_over(values, axis, n):
    return pair_sum(copies(values, axis, n))


def pair_sum(parts):
    while len(parts) > 1:
        parts = [first + second for first, second in zip(parts[::2], parts[1::2])]
    return parts[0]


def sum_and_join(got_ref, small_ref, out_ref):
    small = small_ref[...].astype(BF16)
    for x in range(4):
        total = got_ref[0, x].astype(F32)
        for part in range(1, 4):
            total = total + got_ref[part, x].astype(F32)
        out_ref[x, :576] = total.reshape(576, 128).astype(BF16)
        out_ref[x, 576:] = small


def call_sum_and_join(got, small):
    return pl.pallas_call(
        sum_and_join,
        in_specs=[VMEM] * 2,
        out_specs=VMEM,
        out_shape=S((4, 648, 128), BF16),
        compiler_params=pltpu.CompilerParams(vmem_limit_bytes=40 << 20),
        cost_estimate=FREE,
        name="sum_and_join",
    )(got, small)


def cut_rows(at_ref, got_ref, rows_ref, out_ref):
    total = got_ref[0].astype(F32)
    for part in range(1, 4):
        total = total + got_ref[part].astype(F32)
    extra = total[576:594]
    for quarter in range(1, 4):
        extra = jnp.where(at_ref[0] == quarter, total[576 + 18 * quarter : 594 + 18 * quarter], extra)
    for z in range(8):
        for c in range(9):
            if c < 3:
                block = total[72 * z + 24 * c : 72 * z + 24 * c + 24]
            else:
                block = rows_ref[z, c - 3].astype(F32)
            for quarter in range(4):
                rows = jnp.concatenate([block[6 * quarter : 6 * quarter + 6], extra[2 * c : 2 * c + 2]], axis=0)
                out_ref[4 * z + quarter, c] = rows.astype(BF16)


def call_cut_rows(at, got, rows):
    return pl.pallas_call(
        cut_rows,
        in_specs=[SMEM] + [VMEM] * 2,
        out_specs=VMEM,
        out_shape=S((32, 9, 8, 128), BF16),
        compiler_params=pltpu.CompilerParams(vmem_limit_bytes=40 << 20),
        cost_estimate=pl.CostEstimate(flops=6 * 10**9, bytes_accessed=16 * 10**6, transcendentals=0),
        name="cut_rows",
    )(at, got, rows)


def place_items(at_ref, out_ref, out_other_ref, fg_ref, fg_other_ref, cut_ref, layer_ref, features_ref):
    del at_ref, cut_ref

    @pl.when(pl.program_id(0) == 0)
    def _():
        layer_ref[0] = out_ref[...]
        features_ref[0] = fg_ref[...]

    @pl.when(pl.program_id(0) == 1)
    def _():
        layer_ref[0] = out_other_ref[...]
        features_ref[0] = fg_other_ref[...].astype(F32)


def call_place_items(at, out, out_other, fg, fg_other, cut):
    whole = pl.BlockSpec((L, D), lambda i, at: (0, 0))
    one = pl.BlockSpec((1, L, D), lambda i, at: (at[0] ^ i, 0, 0))
    return pl.pallas_call(
        place_items,
        grid_spec=pltpu.PrefetchScalarGridSpec(
            num_scalar_prefetch=1,
            grid=(2,),
            in_specs=[whole] * 4 + [pl.BlockSpec(memory_space=pl.ANY)],
            out_specs=[one, one],
        ),
        out_shape=[S((2, L, D), BF16), S((2, L, D), F32)],
        compiler_params=pltpu.CompilerParams(vmem_limit_bytes=40 << 20),
        cost_estimate=LONG,
        name="place_items",
    )(at, out, out_other, fg, fg_other, cut)


def on_core(values, at, axis):
    zero = jnp.zeros_like(values)
    return jnp.stack([jnp.where(at["core"] == 0, values, zero), jnp.where(at["core"] == 0, zero, values)], axis=axis)


def pack(query_key_value_weight, out_weight, fc1_weight, fc2_weight):
    kinds = jnp.concatenate(
        [query_key_value_weight.reshape(6, 3, 2, 3, 64), out_weight.T.reshape(6, 1, 2, 3, 64)], axis=1
    ).reshape(6, 2, 2, 2, 3, 64)
    two = kinds[:, :, :, :, :2].reshape(6, 2, 2, 2, 128).transpose(1, 3, 2, 0, 4)
    third = kinds[:, :, :, :, 2].transpose(1, 3, 0, 2, 4).reshape(2, 2, 1, 6, 128)
    first = fc1_weight.reshape(6, 2, 2, 3, 128).transpose(1, 2, 3, 0, 4)
    second = fc2_weight.T.reshape(6, 2, 2, 3, 128).transpose(1, 2, 3, 0, 4)
    return jnp.concatenate([two, third, first, second], axis=2).reshape(4, 9, 6, 128)


def unpack(attention, fc):
    attention = attention.reshape(2, 2, 3, 6, 128)
    two = attention[:, :, :2].reshape(2, 2, 2, 6, 2, 64)
    third = attention[:, :, 2].reshape(2, 2, 6, 2, 64).transpose(0, 1, 3, 2, 4).reshape(2, 2, 2, 6, 1, 64)
    kinds = jnp.concatenate([two, third], axis=4).transpose(0, 2, 3, 1, 4, 5).reshape(4, 6, 384)
    first = fc[:, :3].transpose(2, 0, 1, 3).reshape(6, 1536)
    second = fc[:, 3:].transpose(0, 1, 3, 2).reshape(1536, 6)
    return kinds[:3].transpose(1, 0, 2), kinds[3].T, first, second


def on_device(
    features, patch_counts, ln1_gain, ln1_bias, query_key_value_weight, qv_bias, out_weight, out_bias,
    ln2_gain, ln2_bias, fc1_weight, fc1_bias, fc2_weight, fc2_bias, cotangent,
):
    at = {name: lax.axis_index(name) for name in NAMES}
    at["y"] = at["yh"] * 2 + at["yl"]
    row = lambda v: v.reshape(1, -1)

    rows = gather_rows(pack(query_key_value_weight, out_weight, fc1_weight, fc2_weight))

    item, cot = pick(features, at["yl"]), pick(cotangent, at["yl"])
    item_other, cot_other = swap(item, "core", 2, 1), swap(cot, "core", 2, 1)
    counts = jnp.concatenate([patch_counts, swap(patch_counts, "core", 2, 1), at["yl"].reshape(1)])
    biases = gather(jnp.concatenate([qv_bias.reshape(-1), fc1_bias]).reshape(18, 128), "yl", 2, at["yl"], 0)
    heads_bias = pick(biases[:, :6].reshape(2, 2, 2, 3, 64), at["core"], 2)
    heads_bias = jnp.stack(
        [heads_bias[0, :, :2].reshape(2, 128), heads_bias[1, :, :2].reshape(2, 128), heads_bias[:, :, 2].transpose(1, 0, 2).reshape(2, 128)]
    )
    hidden_bias = pick(biases[:, 6:].reshape(2, 2, 2, 3, 128), at["core"], 2).transpose(2, 1, 0, 3).reshape(3, 1, 512)
    query_bias, value_bias = heads_bias[:, 0], heads_bias[:, 1]
    ob, g1, g2 = row(out_bias), row(ln1_gain), row(ln2_gain)
    rows = whole_rows(after(rows, item_other, cot_other, counts, query_bias, value_bias, hidden_bias))
    low, rest_low, high, rest_high = gather_half(rows, at)
    lows, attention_high = copies(low, Y, 4), exchange(high, "x")
    fc_low, fc_high = lax.all_gather(rest_low, Y), exchange(rest_high, "x")
    n1t, qkv, context, log_total, own, heads = call_forward(
        counts, item, item_other, g1, row(ln1_bias), at["y"].reshape(1), lows, attention_high, query_bias, value_bias
    )
    other = swap(own, "core", 2, 1)
    mlp, mlp_send, gown, hidden_sums, fc_local = call_feed_forward(
        item, item_other, own, other, ob, g2, row(ln2_bias), cot, cot_other,
        fc_low.reshape(4, 2, 3, D // 2, 128), fc_high.reshape(4, 4, 2, 3, 4, 24, 128), hidden_bias
    )
    mid = item.astype(F32) + (own[:L].astype(F32) + other[L:].astype(F32)) + out_bias
    out_rows = (mid + (mlp.astype(F32) + swap(mlp_send, "core", 2, 1).astype(F32)) + fc2_bias).astype(BF16)
    out_other = swap(out_rows, "yl", 2, 1)
    gother = after(swap(gown, "core", 2, 1), out_rows)
    fc = lax.psum_scatter(fc_local.reshape(4, 4, 8, 6, 24, 128), "x")
    grad_mid, sums_two, joined, qv, grads = call_backward(
        counts, item, item_other, own, other, ob, g2, cot, cot_other, gown, gother, heads, qkv, context, log_total, n1t
    )
    got = exchange(after(grads, out_other), Y)
    grad_one, grad_send, sums_one = call_norm_one_grad(item, item_other, heads, joined)

    qv = jnp.concatenate([qv[:2].reshape(2, 2, 2, 64), qv[2].reshape(2, 2, 64).transpose(1, 0, 2)[:, :, None]], axis=2)
    qv = on_core(qv.transpose(1, 0, 2, 3), at, 2).reshape(12, 128)
    hidden_sums = on_core(hidden_sums.reshape(3, 2, 2, 128).transpose(2, 1, 0, 3), at, 2).reshape(24, 128)
    small = jnp.concatenate([sums_one.reshape(12, 128), sums_two.reshape(24, 128), qv, hidden_sums])

    pieces = after(fc, sums_one)
    pieces = [pick(pieces, at["y"] ^ k) for k in range(4)]
    small = small + swap(small, "core", 2, 1)
    parts = copies(small, Y, 4)
    grad_other = after(swap(grad_send, "core", 2, 1), pieces[3])
    fg, fg_low = call_norm_one_back(item, g1, grad_mid, grad_one, grad_other)
    fg_other = swap(fg_low, "yl", 2, 1)
    got = after(got, fg_low)
    parts[1] = after(parts[1], got)
    small = pair_sum(parts)
    got = exchange(call_sum_and_join(got, small), "x")
    pieces = sent(pieces, Y, 4)
    fc_rows = add_up(pieces)
    cut = call_cut_rows((at["yh"] * 2 + at["core"]).reshape(1), got, fc_rows)
    got = jnp.sum(exchange(cut, ROWS).reshape(8, 4, 9, 8, 128).astype(F32), axis=0)
    owned, small = got[:, :, :6], got[:, :, 6:].reshape(72, 128)
    layer_out, features_grad = call_place_items(at["yl"].reshape(1), out_rows, out_other, fg, fg_other, cut)
    qkv_grad, out_grad, fc1_grad, fc2_grad = unpack(owned[:, :3], owned[:, 3:])

    sums = small[:36].reshape(6, D)
    qv_grad = pick(small[36:48].reshape(2, 2, 384), at["yl"], 1)
    hidden_grad = pick(small[48:].reshape(2, 1536), at["yl"])
    return (
        layer_out, features_grad, sums[0], sums[1], qkv_grad, qv_grad, out_grad, sums[2], sums[3], sums[4],
        fc1_grad, hidden_grad, fc2_grad, sums[5],
    )


def solution(mesh):
    five = Mesh(mesh.devices.reshape(SIZES), NAMES)
    return jax.shard_map(
        on_device,
        mesh=five,
        in_specs=(
            P(DP, None, None), P(DP), P(), P(), P(DP, None, "yl"), P(None, "yl"), P("yl", DP), P(),
            P(), P(), P(DP, "yl"), P("yl"), P("yl", DP), P(), P(DP, None, None),
        ),
        out_specs=(
            P(DP, None, None), P(DP, None, None), P(), P(), P(DP, None, "yl"), P(None, "yl"), P("yl", DP), P(),
            P(), P(), P(DP, "yl"), P("yl"), P("yl", DP), P(),
        ),
        check_vma=False,
    )
```

```python
import jax
import jax.numpy as jnp
from jax import lax
from jax.experimental import pallas as pl
from jax.experimental.pallas import tpu as pltpu
from jax.sharding import Mesh, PartitionSpec as P

F32 = jnp.float32
BF16 = jnp.bfloat16
EPS = 1e-06
MASKED = -1e30
VMEM = pl.BlockSpec(memory_space=pltpu.VMEM)
SMEM = pl.BlockSpec(memory_space=pltpu.SMEM)
S = jax.ShapeDtypeStruct
L = 512
D = 768
FREE = pl.CostEstimate(flops=1000, bytes_accessed=1000, transcendentals=0)
LONG = pl.CostEstimate(flops=10**11, bytes_accessed=10**8, transcendentals=0)


def dot_nn(a, b):
    return lax.dot_general(a, b, (((1,), (0,)), ((), ())), preferred_element_type=F32)


def dot_nt(a, b):
    return lax.dot_general(a, b, (((1,), (1,)), ((), ())), preferred_element_type=F32)


def normalize(values):
    row_mean = jnp.mean(values, axis=-1, keepdims=True)
    centred = values - row_mean
    inv_std = lax.rsqrt(jnp.mean(centred * centred, axis=-1, keepdims=True) + EPS)
    return centred * inv_std, inv_std


def norm_back(grad_normed, gain_row, scaled, inv_std):
    grad_scaled = grad_normed * gain_row
    first_mean = jnp.mean(grad_scaled, axis=-1, keepdims=True)
    second_mean = jnp.mean(grad_scaled * scaled, axis=-1, keepdims=True)
    return inv_std * (grad_scaled - first_mean - scaled * second_mean)


def row_sum(values):
    return jnp.sum(values, axis=0, keepdims=True)


def head_lanes(values, head):
    lane = lax.broadcasted_iota(jnp.int32, values.shape, 1)
    return jnp.where((lane >= 64) == (head == 1), values, jnp.zeros_like(values))


def pick_lanes(first, second):
    lane = lax.broadcasted_iota(jnp.int32, first.shape, 1)
    return jnp.where(lane < 64, first, second)


def joined_rows(ref, lead, tail, count):
    return jnp.concatenate([ref[(x, *lead, z, *tail)].astype(F32) for z in range(count) for x in range(4)], axis=0).astype(BF16)


def twist(first, second):
    return (
        jnp.concatenate([first[:, :64], second[:, :64]], axis=1),
        jnp.concatenate([first[:, 64:], second[:, 64:]], axis=1),
    )


def wide(ref, lead, kinds):
    return jnp.concatenate([ref[(*lead, k)] for k in kinds], axis=1)


def forward_attention(count_ref, x_ref, x_other_ref, g1_ref, b1_ref, y_ref, low0_ref, low1_ref, low2_ref, low3_ref, high_ref, qb_ref, vb_ref,
                      n1t_ref, qkv_ref, ctx_ref, lse_ref, part_ref, heads_ref, n1_ref, low_ref):
    for half, ref in enumerate((x_ref, x_other_ref)):
        scaled, _ = normalize(ref[...].astype(F32))
        normed = (scaled * g1_ref[...] + b1_ref[...]).astype(BF16)
        n1_ref[L * half : L * half + L] = normed
        n1t_ref[:, L * half : L * half + L] = normed.T
    for k, ref in enumerate((low0_ref, low1_ref, low2_ref, low3_ref)):
        low_ref[y_ref[0] ^ k] = ref[...]

    def weight(half, p, c):
        return jnp.concatenate([low_ref[2 * half + p, c], joined_rows(high_ref, (2 * half + p, c), (), 4)], axis=0)

    for half in range(2):
        for p in range(2):
            for kind in range(2):
                heads_ref[p, 2 * half + kind] = weight(half, p, kind)
        heads_ref[2, 2 * half], heads_ref[2, 2 * half + 1] = twist(weight(half, 0, 2), weight(half, 1, 2))

    def pair(p, _):
        projected = dot_nn(n1_ref[...], wide(heads_ref, (p,), range(3)))
        queries = (projected[:, :128] + qb_ref[pl.ds(p, 1), :]).astype(BF16) * BF16(0.125)
        keys = projected[:, 128:256].astype(BF16)
        values = (projected[:, 256:] + vb_ref[pl.ds(p, 1), :]).astype(BF16)
        qkv_ref[0, p] = queries
        qkv_ref[1, p] = keys
        qkv_ref[2, p] = values
        for item in range(2):
            rows = slice(L * item, L * item + L)
            query, key, value_t = queries[rows], keys[rows], values[rows].T
            valid = lax.broadcasted_iota(jnp.int32, (L, L), 0) < count_ref[2 * item + count_ref[4]]
            parts = []
            for head in range(2):
                scores = jnp.where(valid, dot_nt(head_lanes(key, head), query), MASKED)
                top = jnp.max(scores, axis=0, keepdims=True)
                shifted = jnp.exp(scores - top)
                total = row_sum(shifted)
                prob = shifted * (1.0 / total)
                parts.append(dot_nn(value_t[64 * head : 64 * head + 64], prob.astype(BF16)))
                lse_ref[p, item, pl.ds(head, 1), :] = top + jnp.log(total)
            ctx_ref[p, rows] = jnp.concatenate(parts, axis=0).T.astype(BF16)
        return 0

    lax.fori_loop(0, 3, pair, 0)
    context = jnp.concatenate([ctx_ref[p] for p in range(3)], axis=1)
    for j in range(3):
        cols = slice(256 * j, 256 * j + 256)
        out = jnp.concatenate([heads_ref[p, 3, cols, :] for p in range(3)], axis=1)
        part_ref[:, cols] = dot_nt(context, out).astype(BF16)


def call_forward(counts, x, x_other, g1, b1, y, lows, high, qb, vb):
    rows = 2 * L
    return pl.pallas_call(
        forward_attention,
        in_specs=[SMEM] + [VMEM] * 4 + [SMEM] + [VMEM] * 7,
        out_specs=[VMEM] * 6,
        out_shape=[S((D, rows), BF16), S((3, 3, rows, 128), BF16), S((3, rows, 128), BF16),
                   S((3, 2, 2, L), F32), S((rows, D), BF16), S((3, 4, D, 128), BF16)],
        scratch_shapes=[pltpu.VMEM((rows, D), BF16), pltpu.VMEM((4, 3, D // 2, 128), BF16)],
        compiler_params=pltpu.CompilerParams(vmem_limit_bytes=50 << 20),
        cost_estimate=FREE,
        name="attention_forward",
    )(counts, x, x_other, g1, b1, y, *lows, high, qb, vb)


def middle(x_refs, own_ref, other_ref, ob_ref, half):
    mine, theirs = pl.ds(L * half, L), pl.ds(L - L * half, L)
    return x_refs[half][...].astype(F32) + (own_ref[mine, :].astype(F32) + other_ref[theirs, :].astype(F32)) + ob_ref[...]


def feed_forward(x_ref, x_other_ref, own_ref, other_ref, ob_ref, g2_ref, b2_ref, cot_ref, cot_other_ref, low_ref, high_ref, b1_ref,
                 mlp_ref, mlp_send_ref, gn2_ref, db_ref, dw_ref, n2_ref, n2t_ref, cots_ref, cott_ref, acc_ref, gacc_ref):
    step = pl.program_id(0)
    last = pl.num_programs(0) - 1

    @pl.when(step == 0)
    def _():
        for half in range(2):
            scaled, _ = normalize(middle((x_ref, x_other_ref), own_ref, other_ref, ob_ref, half))
            n2_ref[L * half : L * half + L] = (scaled * g2_ref[...] + b2_ref[...]).astype(BF16)
            cots_ref[L * half : L * half + L] = (cot_ref, cot_other_ref)[half][...]
        n2t_ref[...] = n2_ref[...].T
        cott_ref[...] = cots_ref[...].T
        acc_ref[...] = jnp.zeros_like(acc_ref)
        gacc_ref[...] = jnp.zeros_like(gacc_ref)

    first, second = (
        jnp.concatenate(
            [jnp.concatenate([low_ref[y, layer, 0], joined_rows(high_ref, (y, layer, 0), (), 4)], axis=0) for y in range(4)], axis=1
        )
        for layer in range(2)
    )
    hidden = dot_nn(n2_ref[...], first) + b1_ref[0]
    cdf = 0.5 * (1.0 + lax.erf(hidden * 0.7071067811865476))
    slope = cdf + hidden * (jnp.exp(-0.5 * hidden * hidden) * 0.3989422804014327)
    active = (hidden * cdf).astype(BF16)
    acc_ref[...] += dot_nt(active, second)
    grad_hidden = dot_nn(cots_ref[...], second) * slope
    db_ref[0] = row_sum(grad_hidden)
    grad_hidden = grad_hidden.astype(BF16)
    gacc_ref[...] += dot_nt(grad_hidden, first)
    for layer, grad in enumerate((dot_nn(n2t_ref[...], grad_hidden), dot_nn(cott_ref[...], active))):
        for x in range(4):
            for z in range(8):
                block = grad[96 * z + 24 * x : 96 * z + 24 * x + 24].astype(BF16)
                for y in range(4):
                    dw_ref[x, y, z, layer, 0] = block[:, 128 * y : 128 * y + 128]

    @pl.when(step == last)
    def _():
        mlp_ref[...] = acc_ref[:L].astype(BF16)
        mlp_send_ref[...] = acc_ref[L:].astype(BF16)
        gn2_ref[...] = gacc_ref[...].astype(BF16)


def call_feed_forward(x, x_other, own, other, ob, g2, b2, cot, cot_other, low, high, b1):
    rows = 2 * L
    half = pl.BlockSpec((L, D), lambda i: (0, 0))
    whole = pl.BlockSpec((rows, D), lambda i: (0, 0))
    line = pl.BlockSpec((1, D), lambda i: (0, 0))
    lows = pl.BlockSpec((4, 2, 1, D // 2, 128), lambda i: (0, 0, i, 0, 0))
    highs = pl.BlockSpec((4, 4, 2, 1, 4, 24, 128), lambda i: (0, 0, 0, i, 0, 0, 0))
    grads = pl.BlockSpec((4, 4, 8, 2, 1, 24, 128), lambda i: (0, 0, 0, 0, i, 0, 0))
    bias = pl.BlockSpec((1, 1, 512), lambda i: (i, 0, 0))
    return pl.pallas_call(
        feed_forward,
        grid=(3,),
        in_specs=[half, half, whole, whole, line, line, line, half, half, lows, highs, bias],
        out_specs=[half, half, whole, bias, grads],
        out_shape=[S((L, D), BF16), S((L, D), BF16), S((rows, D), BF16), S((3, 1, 512), F32), S((4, 4, 8, 2, 3, 24, 128), BF16)],
        scratch_shapes=[pltpu.VMEM((rows, D), BF16), pltpu.VMEM((D, rows), BF16), pltpu.VMEM((rows, D), BF16),
                        pltpu.VMEM((D, rows), BF16), pltpu.VMEM((rows, D), F32), pltpu.VMEM((rows, D), F32)],
        compiler_params=pltpu.CompilerParams(vmem_limit_bytes=58 << 20),
        cost_estimate=FREE,
        name="feed_forward",
    )(x, x_other, own, other, ob, g2, b2, cot, cot_other, low, high, b1)


def norm_two_back(x_refs, own_ref, other_ref, ob_ref, g2_ref, cot_refs, gown_ref, gother_ref, gb_ref, gbt_ref, gm_ref, sums_ref):
    for half in range(2):
        mine, theirs = pl.ds(L * half, L), pl.ds(L - L * half, L)
        scaled, inv = normalize(middle(x_refs, own_ref, other_ref, ob_ref, half))
        grad = gown_ref[mine, :].astype(F32) + gother_ref[theirs, :].astype(F32)
        cot = cot_refs[half][...].astype(F32)
        grad_mid = cot + norm_back(grad, g2_ref[...], scaled, inv)
        branch = grad_mid.astype(BF16)
        gb_ref[mine, :] = branch
        gbt_ref[:, L * half : L * half + L] = branch.T
        if half == 0:
            gm_ref[...] = grad_mid
            sums_ref[0:1, :] = row_sum(branch.astype(F32))
            sums_ref[1:2, :] = row_sum(grad * scaled)
            sums_ref[2:3, :] = row_sum(grad)
            sums_ref[3:4, :] = row_sum(cot)


def backward_pair(p, count_ref, heads_ref, qkv_ref, ctx_ref, lse_ref, gb_ref, gbt_ref, n1t_ref, joined_ref, qvb_ref):
    grad_context = dot_nn(gb_ref[...], heads_ref[p, 3]).astype(BF16)
    grad_out = dot_nn(gbt_ref[...], ctx_ref[p])
    for item in range(2):
        rows = slice(L * item, L * item + L)
        query, key, value = qkv_ref[0, p, rows], qkv_ref[1, p, rows], qkv_ref[2, p, rows]
        grad_ctx = grad_context[rows]
        key_t = key.T
        valid = lax.broadcasted_iota(jnp.int32, (L, L), 0) < count_ref[2 * item + count_ref[4]]
        grad_q, grad_k, grad_v = [], [], []
        for head in range(2):
            scores = jnp.where(valid, dot_nt(head_lanes(key, head), query), MASKED)
            prob = jnp.exp(scores - lse_ref[p, item, pl.ds(head, 1), :])
            grad_prob = dot_nt(head_lanes(value, head), grad_ctx)
            delta = row_sum(prob * grad_prob)
            grad_scores = (prob * (grad_prob - delta)).astype(BF16)
            grad_k.append(dot_nn(grad_scores, query))
            grad_v.append(dot_nn(prob.astype(BF16), grad_ctx))
            grad_q.append(dot_nn(key_t[64 * head : 64 * head + 64], grad_scores))
        joined_ref[p, rows, 0:128] = (jnp.concatenate(grad_q, axis=0).T * 0.125).astype(BF16)
        joined_ref[p, rows, 128:256] = pick_lanes(*grad_k).astype(BF16)
        joined_ref[p, rows, 256:384] = pick_lanes(*grad_v).astype(BF16)
    joined = joined_ref[p]
    sums = row_sum(joined.astype(F32))
    qvb_ref[p, 0:1, :] = sums[:, :128]
    qvb_ref[p, 1:2, :] = sums[:, 256:]
    grads = dot_nn(n1t_ref[...], joined)
    return grads[:, :128], grads[:, 128:256], grads[:, 256:], grad_out


def backward_attention(count_ref, x_ref, x_other_ref, own_ref, other_ref, ob_ref, g2_ref, cot_ref, cot_other_ref, gown_ref, gother_ref,
                       heads_ref, qkv_ref, ctx_ref, lse_ref, n1t_ref,
                       gm_ref, sums_ref, joined_ref, qvb_ref, dw_ref, gb_ref, gbt_ref, last_ref):
    norm_two_back((x_ref, x_other_ref), own_ref, other_ref, ob_ref, g2_ref, (cot_ref, cot_other_ref), gown_ref, gother_ref,
                  gb_ref, gbt_ref, gm_ref, sums_ref)

    def pair(p, _):
        grads = backward_pair(p, count_ref, heads_ref, qkv_ref, ctx_ref, lse_ref, gb_ref, gbt_ref, n1t_ref, joined_ref, qvb_ref)

        @pl.when(p < 2)
        def _():
            for i, grad in enumerate(grads):
                spread(dw_ref, 2 * (i // 2) + p, i % 2, grad)

        @pl.when(p == 2)
        def _():
            for i, grad in enumerate(grads):
                last_ref[i] = grad

        return 0

    lax.fori_loop(0, 3, pair, 0)
    for high in range(2):
        for low, grad in enumerate(twist(last_ref[2 * high], last_ref[2 * high + 1])):
            spread(dw_ref, 2 * high + low, 2, grad)


def spread(dw_ref, y, c, grad):
    for z in range(8):
        for x in range(4):
            at = 24 * (4 * z + x)
            dw_ref[y, x, z, c] = grad[at : at + 24].astype(BF16)


def call_backward(counts, x, x_other, own, other, ob, g2, cot, cot_other, gown, gother, heads, qkv, ctx, lse, n1t):
    rows = 2 * L
    return pl.pallas_call(
        backward_attention,
        in_specs=[SMEM] + [VMEM] * 15,
        out_specs=[VMEM] * 5,
        out_shape=[S((L, D), F32), S((4, D), F32), S((3, rows, 384), BF16), S((3, 2, 128), F32), S((4, 4, 8, 3, 24, 128), BF16)],
        scratch_shapes=[pltpu.VMEM((rows, D), BF16), pltpu.VMEM((D, rows), BF16), pltpu.VMEM((4, D, 128), F32)],
        compiler_params=pltpu.CompilerParams(vmem_limit_bytes=58 << 20),
        cost_estimate=FREE,
        name="attention_backward",
    )(counts, x, x_other, own, other, ob, g2, cot, cot_other, gown, gother, heads, qkv, ctx, lse, n1t)


def norm_one_grad(x_ref, x_other_ref, heads_ref, joined_ref, own_ref, send_ref, sums_ref):
    for half in range(2):
        rows = slice(L * half, L * half + L)
        grad = dot_nt(joined_ref[0, rows, :], wide(heads_ref, (0,), range(3)))
        for p in range(1, 3):
            grad = grad + dot_nt(joined_ref[p, rows, :], wide(heads_ref, (p,), range(3)))
        scaled, _ = normalize((x_ref, x_other_ref)[half][...].astype(F32))
        if half == 0:
            own_ref[...] = grad
            gain, shift = row_sum(grad * scaled), row_sum(grad)
        else:
            send_ref[...] = grad.astype(BF16)
            sums_ref[0:1, :] = gain + row_sum(grad * scaled)
            sums_ref[1:2, :] = shift + row_sum(grad)


def call_norm_one_grad(x, x_other, heads, joined):
    return pl.pallas_call(
        norm_one_grad,
        in_specs=[VMEM] * 4,
        out_specs=[VMEM] * 3,
        out_shape=[S((L, D), F32), S((L, D), BF16), S((2, D), F32)],
        compiler_params=pltpu.CompilerParams(vmem_limit_bytes=50 << 20),
        cost_estimate=FREE,
        name="norm_one_grad",
    )(x, x_other, heads, joined)


def norm_one_back(x_ref, g1_ref, gm_ref, own_ref, other_ref, fg_ref, low_ref):
    scaled, inv = normalize(x_ref[...].astype(F32))
    grad = own_ref[...] + other_ref[...].astype(F32)
    result = gm_ref[...] + norm_back(grad, g1_ref[...], scaled, inv)
    fg_ref[...] = result
    low_ref[...] = result.astype(BF16)


def call_norm_one_back(x, g1, gm, own, other):
    return pl.pallas_call(
        norm_one_back,
        grid=(1,),
        in_specs=[pl.BlockSpec((L, D), lambda i: (0, 0)), pl.BlockSpec((1, D), lambda i: (0, 0))]
        + [pl.BlockSpec((L, D), lambda i: (0, 0))] * 3,
        out_specs=[pl.BlockSpec((L, D), lambda i: (0, 0))] * 2,
        out_shape=[S((L, D), F32), S((L, D), BF16)],
        compiler_params=pltpu.CompilerParams(vmem_limit_bytes=40 << 20),
        cost_estimate=FREE,
        name="norm_one_back",
    )(x, g1, gm, own, other)


NAMES = ("z", "x", "yh", "core", "yl")
SIZES = (8, 4, 2, 2, 2)
DP = ("z", "x", "yh", "core")
Y = ("yh", "yl")
QUARTER = ("yh", "core")
ROWS = ("z", "yh", "core")


def after(values, *earlier):
    return pl.pallas_call(
        lambda *refs: None,
        in_specs=[pl.BlockSpec(memory_space=pl.ANY)] * (1 + len(earlier)),
        out_specs=pl.BlockSpec(memory_space=pl.ANY),
        out_shape=S(values.shape, values.dtype),
        input_output_aliases={0: 0},
        cost_estimate=FREE,
        name="after",
    )(values, *earlier)


def swap(values, axis, n, k):
    return lax.ppermute(values, axis, [(i, i ^ k) for i in range(n)])


def pick(values, index, axis=0):
    return lax.dynamic_index_in_dim(values, index, axis, keepdims=False)


def in_order(parts, index, axis):
    bit = 1
    while bit < len(parts):
        flip = (index & bit) != 0
        parts = [jnp.where(flip, parts[k ^ bit], parts[k]) for k in range(len(parts))]
        bit *= 2
    return jnp.stack(parts, axis=axis)


def gather(values, axis, n, index, place):
    return in_order([values] + [swap(values, axis, n, k) for k in range(1, n)], index, place)


def add_up(parts):
    total = parts[0].astype(F32)
    for part in parts[1:]:
        total = total + part.astype(F32)
    return total.astype(BF16)


def sent(parts, axis, n):
    return [parts[0]] + [swap(parts[k], axis, n, k) for k in range(1, n)]


def gather_rows(packed):
    c = packed.shape[1]
    return exchange(repeated(packed, 8).reshape(32, c, 6, 128), ROWS).reshape(8, 4, c, 6, 128)


def whole_rows(got):
    return got.transpose(2, 0, 1, 3, 4).reshape(got.shape[2], 8, 24, 128)


def copies(values, axis, n):
    return [values] + [swap(values, axis, n, k) for k in range(1, n)]


def assemble(at_ref, *refs):
    lows, highs, (low_ref, rest_low_ref, high_ref, rest_high_ref) = refs[:4], refs[4:8], refs[8:]
    for k in range(4):
        x, y = at_ref[0] ^ k, at_ref[1] ^ k
        low_ref[:, :, x] = lows[k][:3]
        rest_low_ref[:, :, x] = lows[k][3:]
        for copy in range(4):
            high_ref[copy, y] = highs[k][:3]
            rest_high_ref[copy, y] = highs[k][3:]


def gather_half(rows, at):
    parts = copies(rows[:, :4], "x", 4) + copies(rows[:, 4:], Y, 4)
    low, rest_low, high, rest_high = pl.pallas_call(
        assemble,
        in_specs=[SMEM] + [VMEM] * 8,
        out_specs=[VMEM] * 4,
        out_shape=[S((3, 4, 4, 24, 128), BF16), S((6, 4, 4, 24, 128), BF16),
                   S((4, 4, 3, 4, 24, 128), BF16), S((4, 4, 6, 4, 24, 128), BF16)],
        compiler_params=pltpu.CompilerParams(vmem_limit_bytes=40 << 20),
        cost_estimate=FREE,
        name="assemble",
    )(jnp.stack([at["x"], at["y"]]), *parts)
    return low.reshape(3, 384, 128), rest_low.reshape(6, 384, 128), high, rest_high


def repeated(values, n):
    return jnp.broadcast_to(values[None], (n, *values.shape))


def exchange(values, axis):
    return lax.all_to_all(values, axis, split_axis=0, concat_axis=0, tiled=True)


def sum_over(values, axis, n):
    return pair_sum(copies(values, axis, n))


def pair_sum(parts):
    while len(parts) > 1:
        parts = [first + second for first, second in zip(parts[::2], parts[1::2])]
    return parts[0]


def sum_and_join(got_ref, small_ref, out_ref):
    small = small_ref[...].astype(BF16)
    for x in range(4):
        total = got_ref[0, x].astype(F32)
        for part in range(1, 4):
            total = total + got_ref[part, x].astype(F32)
        out_ref[x, :576] = total.reshape(576, 128).astype(BF16)
        out_ref[x, 576:] = small


def call_sum_and_join(got, small):
    return pl.pallas_call(
        sum_and_join,
        in_specs=[VMEM] * 2,
        out_specs=VMEM,
        out_shape=S((4, 648, 128), BF16),
        compiler_params=pltpu.CompilerParams(vmem_limit_bytes=40 << 20),
        cost_estimate=FREE,
        name="sum_and_join",
    )(got, small)


def cut_rows(at_ref, got_ref, first_ref, second_ref, third_ref, fourth_ref, out_ref):
    total = got_ref[0].astype(F32)
    for part in range(1, 4):
        total = total + got_ref[part].astype(F32)
    extra = total[576:594]
    for quarter in range(1, 4):
        extra = jnp.where(at_ref[0] == quarter, total[576 + 18 * quarter : 594 + 18 * quarter], extra)
    for z in range(8):
        for c in range(9):
            if c < 3:
                block = total[72 * z + 24 * c : 72 * z + 24 * c + 24]
            else:
                block = first_ref[z, c - 3].astype(F32)
                for ref in (second_ref, third_ref, fourth_ref):
                    block = block + ref[z, c - 3].astype(F32)
            for quarter in range(4):
                rows = jnp.concatenate([block[6 * quarter : 6 * quarter + 6], extra[2 * c : 2 * c + 2]], axis=0)
                out_ref[4 * z + quarter, c] = rows.astype(BF16)


def call_cut_rows(at, got, pieces):
    return pl.pallas_call(
        cut_rows,
        in_specs=[SMEM] + [VMEM] * 5,
        out_specs=VMEM,
        out_shape=S((32, 9, 8, 128), BF16),
        compiler_params=pltpu.CompilerParams(vmem_limit_bytes=40 << 20),
        cost_estimate=pl.CostEstimate(flops=6 * 10**9, bytes_accessed=16 * 10**6, transcendentals=0),
        name="cut_rows",
    )(at, got, *pieces)


def place_items(at_ref, out_ref, out_other_ref, fg_ref, fg_other_ref, cut_ref, layer_ref, features_ref):
    del at_ref, cut_ref

    @pl.when(pl.program_id(0) == 0)
    def _():
        layer_ref[0] = out_ref[...]
        features_ref[0] = fg_ref[...]

    @pl.when(pl.program_id(0) == 1)
    def _():
        layer_ref[0] = out_other_ref[...]
        features_ref[0] = fg_other_ref[...].astype(F32)


def call_place_items(at, out, out_other, fg, fg_other, cut):
    whole = pl.BlockSpec((L, D), lambda i, at: (0, 0))
    one = pl.BlockSpec((1, L, D), lambda i, at: (at[0] ^ i, 0, 0))
    return pl.pallas_call(
        place_items,
        grid_spec=pltpu.PrefetchScalarGridSpec(
            num_scalar_prefetch=1,
            grid=(2,),
            in_specs=[whole] * 4 + [pl.BlockSpec(memory_space=pl.ANY)],
            out_specs=[one, one],
        ),
        out_shape=[S((2, L, D), BF16), S((2, L, D), F32)],
        compiler_params=pltpu.CompilerParams(vmem_limit_bytes=40 << 20),
        cost_estimate=LONG,
        name="place_items",
    )(at, out, out_other, fg, fg_other, cut)


def on_core(values, at, axis):
    zero = jnp.zeros_like(values)
    return jnp.stack([jnp.where(at["core"] == 0, values, zero), jnp.where(at["core"] == 0, zero, values)], axis=axis)


def pack(query_key_value_weight, out_weight, fc1_weight, fc2_weight):
    kinds = jnp.concatenate(
        [query_key_value_weight.reshape(6, 3, 2, 3, 64), out_weight.T.reshape(6, 1, 2, 3, 64)], axis=1
    ).reshape(6, 2, 2, 2, 3, 64)
    two = kinds[:, :, :, :, :2].reshape(6, 2, 2, 2, 128).transpose(1, 3, 2, 0, 4)
    third = kinds[:, :, :, :, 2].transpose(1, 3, 0, 2, 4).reshape(2, 2, 1, 6, 128)
    first = fc1_weight.reshape(6, 2, 2, 3, 128).transpose(1, 2, 3, 0, 4)
    second = fc2_weight.T.reshape(6, 2, 2, 3, 128).transpose(1, 2, 3, 0, 4)
    return jnp.concatenate([two, third, first, second], axis=2).reshape(4, 9, 6, 128)


def unpack(attention, fc):
    attention = attention.reshape(2, 2, 3, 6, 128)
    two = attention[:, :, :2].reshape(2, 2, 2, 6, 2, 64)
    third = attention[:, :, 2].reshape(2, 2, 6, 2, 64).transpose(0, 1, 3, 2, 4).reshape(2, 2, 2, 6, 1, 64)
    kinds = jnp.concatenate([two, third], axis=4).transpose(0, 2, 3, 1, 4, 5).reshape(4, 6, 384)
    first = fc[:, :3].transpose(2, 0, 1, 3).reshape(6, 1536)
    second = fc[:, 3:].transpose(0, 1, 3, 2).reshape(1536, 6)
    return kinds[:3].transpose(1, 0, 2), kinds[3].T, first, second


def on_device(
    features, patch_counts, ln1_gain, ln1_bias, query_key_value_weight, qv_bias, out_weight, out_bias,
    ln2_gain, ln2_bias, fc1_weight, fc1_bias, fc2_weight, fc2_bias, cotangent,
):
    at = {name: lax.axis_index(name) for name in NAMES}
    at["y"] = at["yh"] * 2 + at["yl"]
    row = lambda v: v.reshape(1, -1)

    rows = gather_rows(pack(query_key_value_weight, out_weight, fc1_weight, fc2_weight))

    item, cot = pick(features, at["yl"]), pick(cotangent, at["yl"])
    item_other, cot_other = swap(item, "core", 2, 1), swap(cot, "core", 2, 1)
    counts = jnp.concatenate([patch_counts, swap(patch_counts, "core", 2, 1), at["yl"].reshape(1)])
    biases = gather(jnp.concatenate([qv_bias.reshape(-1), fc1_bias]).reshape(18, 128), "yl", 2, at["yl"], 0)
    heads_bias = pick(biases[:, :6].reshape(2, 2, 2, 3, 64), at["core"], 2)
    heads_bias = jnp.stack(
        [heads_bias[0, :, :2].reshape(2, 128), heads_bias[1, :, :2].reshape(2, 128), heads_bias[:, :, 2].transpose(1, 0, 2).reshape(2, 128)]
    )
    hidden_bias = pick(biases[:, 6:].reshape(2, 2, 2, 3, 128), at["core"], 2).transpose(2, 1, 0, 3).reshape(3, 1, 512)
    query_bias, value_bias = heads_bias[:, 0], heads_bias[:, 1]
    ob, g1, g2 = row(out_bias), row(ln1_gain), row(ln2_gain)
    rows = whole_rows(after(rows, item_other, cot_other, counts, query_bias, value_bias, hidden_bias))
    low, rest_low, high, rest_high = gather_half(rows, at)
    lows, attention_high = copies(low, Y, 4), exchange(high, "x")
    fc_low, fc_high = lax.all_gather(rest_low, Y), exchange(rest_high, "x")
    n1t, qkv, context, log_total, own, heads = call_forward(
        counts, item, item_other, g1, row(ln1_bias), at["y"].reshape(1), lows, attention_high, query_bias, value_bias
    )
    other = swap(own, "core", 2, 1)
    mlp, mlp_send, gown, hidden_sums, fc_local = call_feed_forward(
        item, item_other, own, other, ob, g2, row(ln2_bias), cot, cot_other,
        fc_low.reshape(4, 2, 3, D // 2, 128), fc_high.reshape(4, 4, 2, 3, 4, 24, 128), hidden_bias
    )
    mid = item.astype(F32) + (own[:L].astype(F32) + other[L:].astype(F32)) + out_bias
    out_rows = (mid + (mlp.astype(F32) + swap(mlp_send, "core", 2, 1).astype(F32)) + fc2_bias).astype(BF16)
    out_other = swap(out_rows, "yl", 2, 1)
    gother = after(swap(gown, "core", 2, 1), out_rows)
    fc = lax.psum_scatter(fc_local.reshape(4, 4, 8, 6, 24, 128), "x")
    grad_mid, sums_two, joined, qv, grads = call_backward(
        counts, item, item_other, own, other, ob, g2, cot, cot_other, gown, gother, heads, qkv, context, log_total, n1t
    )
    got = exchange(after(grads, out_other), Y)
    grad_one, grad_send, sums_one = call_norm_one_grad(item, item_other, heads, joined)

    qv = jnp.concatenate([qv[:2].reshape(2, 2, 2, 64), qv[2].reshape(2, 2, 64).transpose(1, 0, 2)[:, :, None]], axis=2)
    qv = on_core(qv.transpose(1, 0, 2, 3), at, 2).reshape(12, 128)
    hidden_sums = on_core(hidden_sums.reshape(3, 2, 2, 128).transpose(2, 1, 0, 3), at, 2).reshape(24, 128)
    small = jnp.concatenate([sums_one.reshape(12, 128), sums_two.reshape(24, 128), qv, hidden_sums])

    pieces = after(fc, sums_one)
    pieces = [pick(pieces, at["y"] ^ k) for k in range(4)]
    small = small + swap(small, "core", 2, 1)
    parts = copies(small, Y, 4)
    grad_other = after(swap(grad_send, "core", 2, 1), pieces[3])
    fg, fg_low = call_norm_one_back(item, g1, grad_mid, grad_one, grad_other)
    fg_other = swap(fg_low, "yl", 2, 1)
    got = after(got, fg_low)
    parts[1] = after(parts[1], got)
    small = pair_sum(parts)
    got = exchange(call_sum_and_join(got, small), "x")
    pieces = sent(pieces, Y, 4)
    cut = call_cut_rows((at["yh"] * 2 + at["core"]).reshape(1), got, pieces)
    got = jnp.sum(exchange(cut, ROWS).reshape(8, 4, 9, 8, 128).astype(F32), axis=0)
    owned, small = got[:, :, :6], got[:, :, 6:].reshape(72, 128)
    layer_out, features_grad = call_place_items(at["yl"].reshape(1), out_rows, out_other, fg, fg_other, cut)
    qkv_grad, out_grad, fc1_grad, fc2_grad = unpack(owned[:, :3], owned[:, 3:])

    sums = small[:36].reshape(6, D)
    qv_grad = pick(small[36:48].reshape(2, 2, 384), at["yl"], 1)
    hidden_grad = pick(small[48:].reshape(2, 1536), at["yl"])
    return (
        layer_out, features_grad, sums[0], sums[1], qkv_grad, qv_grad, out_grad, sums[2], sums[3], sums[4],
        fc1_grad, hidden_grad, fc2_grad, sums[5],
    )


def solution(mesh):
    five = Mesh(mesh.devices.reshape(SIZES), NAMES)
    return jax.shard_map(
        on_device,
        mesh=five,
        in_specs=(
            P(DP, None, None), P(DP), P(), P(), P(DP, None, "yl"), P(None, "yl"), P("yl", DP), P(),
            P(), P(), P(DP, "yl"), P("yl"), P("yl", DP), P(), P(DP, None, None),
        ),
        out_specs=(
            P(DP, None, None), P(DP, None, None), P(), P(), P(DP, None, "yl"), P(None, "yl"), P("yl", DP), P(),
            P(), P(), P(DP, "yl"), P("yl"), P("yl", DP), P(),
        ),
        check_vma=False,
    )
```
